32 devices in a mesh: trade: 8 (over z, y), scen: 4 (over x, core).
Axes of the slice: x: 2, y: 2, z: 4, core: 2. Of those that a mesh axis runs over, the one named last changes fastest.
Arguments:
- log_vol: float32 [256, 2048], P('trade'), may hold values from -2.3 to -0.5
- beta: float32 [256], P('trade'), may hold values from 0.5 to 2
- shock_table: bfloat16 [512, 2048], replicated, may hold values from -0.29882812 to 0.3984375
- scen_ids: int32 [8], P('scen'), may hold values from 0 to 511
- hot_index: int32 [16], P('trade'), may hold values from 0 to 31
- dest: int32 [65536, 1], P('trade'), may hold values from 0 to 7; in each aligned block of 2048 rows (0 to 2047, 2048 to 4095, ...) at most 512 rows name the same one
- pick: int32 [65536], P('trade'), may hold values from 0 to 35
- expiry_cell: int32 [65536], P('trade'), may hold values from 1 to 61
- strike_cell: int32 [65536], P('trade'), may hold values from 1 to 29
- frac_e: float32 [65536], P('trade'), may hold values from 0 to 1
- frac_k: float32 [65536], P('trade'), may hold values from 0 to 1
- notional: float32 [65536], P('trade'), may hold values from -12 to 12
- forward: float32 [65536], P('trade'), may hold values from 0.5 to 2
Outputs:
- price_out: float32 [8, 65536], P('scen', 'trade')
- vega_out: float32 [8, 65536], P('scen', 'trade')
- delta_out: float32 [8, 65536], P('scen', 'trade')
The draws below stay inside these ranges and needn't reach their ends.
Inputs may be any that keep to these rules, and one draw needn't show every extreme that they name: `dest`: within each aligned block of 2048 trades no device is named by more than 512 trades, and some device is named exactly 512 times.
All inputs are finite; a program needn't handle non-finite values.
Results may differ from the reference program's by a relative error of at most 0.0031.
Values may be sent and summed in bfloat16 or wider, within the bound.
No kernel may reach another device: no remote copies, remote signals or barrier semaphores. Data moves between devices by JAX's collectives and lax.ppermute only.
A program may use at most 128 MiB of HBM per device.

```python
import math
import jax
import jax.numpy as jnp
import numpy as np
from jax import lax

NE = 64
NK = 32
NSHOCK = 512
SCEN = 8
HOT = 2
U_DEV = 32
TR_SUB = 2048
CAP = 512
TRADES = 65536
U = 256
HOTS = 16
HELD = 36
N_TRADE = 8


def set_ends(result, own_key, smallest, largest):
    place = [jax.random.randint(jax.random.fold_in(own_key, axis), (), 0, length) for axis, length in enumerate(result.shape)]
    longest = result.shape.index(max(result.shape))
    beside = place[:longest] + [(place[longest] + 1) % result.shape[longest]] + place[longest + 1:]
    return result.at[tuple(place)].set(smallest).at[tuple(beside)].set(largest)


def levels(rng, shape, split, smallest, top_value):
    level, own = 1.0, jax.random.fold_in(rng, 6)
    for dim, parts in split:
        draws = jnp.exp(jax.random.uniform(jax.random.fold_in(own, dim), (parts,), jnp.float32, smallest / len(split), top_value / len(split)))
        level = level * jnp.repeat(draws, shape[dim] // parts).reshape([-1 if axis == dim else 1 for axis in range(len(shape))])
    return level


def routed_block(key, own, number, rows, amount, top, bound, skew):
    order = jax.random.permutation(key, amount)
    packed, common = load_shares(amount, rows * top, bound, skew, True), load_shares(amount, rows * top, bound, skew, False)
    places = jnp.arange(amount)

    def named(sizes, turn):
        used = int((sizes > 0).sum())
        fixed = max(1, used // 4)
        moved = fixed + (places - fixed + turn * (used - fixed)) % max(1, amount - fixed)
        return jnp.zeros((amount,), jnp.int32).at[order[jnp.where(places < fixed, places, moved)]].set(jnp.asarray(sizes, jnp.int32))

    sizes = jnp.where(number % 4 == 0, named(packed, number // 4), named(common, number - number // 4 - 1))
    mixed = jax.random.permutation(jax.random.fold_in(own, 3), amount)
    giver, sink = mixed[0:amount // 2 * 2:2], mixed[1:amount // 2 * 2:2]
    margin = jnp.minimum(sizes[giver] - 1, bound - sizes[sink]) // 2
    margin = jnp.where((giver == order[0]) | (sink == order[0]) | (sizes[sink] == 0), 0, jnp.maximum(margin, 0))
    moved = jax.random.randint(jax.random.fold_in(own, 4), (amount // 2,), 0, 1 << 20) % (margin + 1)
    sizes = sizes.at[giver].add(-moved).at[sink].add(moved)
    members = jnp.searchsorted(jnp.cumsum(sizes), jnp.arange(rows * top), side="right").astype(jnp.int32)
    grid = members.reshape(top, rows).T
    grid = grid[jax.random.permutation(jax.random.fold_in(own, 1), rows)]
    turn = jax.random.randint(jax.random.fold_in(own, 2), (rows, 1), 0, top)
    return jnp.take_along_axis(grid, (jnp.arange(top)[None, :] + turn) % top, axis=1)


def load_shares(number_of, total, bound, skew, full):
    weights = [(1 << 20) // math.isqrt(rank ** skew) + 1 for rank in range(1, number_of + 1)]
    largest = bound if full else min(bound, max(-(-total // number_of), total * weights[0] // sum(weights)))
    least = 1 if total - largest >= number_of - 1 else 0
    holding, surplus = [largest] + [least] * (number_of - 1), total - largest - least * (number_of - 1)
    while surplus > 0:
        free = [i for i in range(1, number_of) if holding[i] < largest] or [i for i in range(1, number_of) if holding[i] < bound]
        mass, remaining = sum([weights[i] for i in free]), surplus
        for i in free:
            more = min(bound - holding[i], max(1, remaining * weights[i] // mass), surplus)
            holding[i] = holding[i] + more
            surplus = surplus - more
    return np.array(holding)


def normal_values(rng, extent, width, most, pieces=(), dtype=jnp.bfloat16):
    gain = levels(rng, extent, pieces, -0.22, 0.18) if pieces else 1.0
    entries = jax.random.normal(rng, extent, jnp.float32) * width * gain
    return jnp.minimum(jnp.maximum(entries, -most), most).astype(dtype)


def setup_inputs(seed: int = 0) -> dict:
    streams_of = jax.random.split(jax.random.key(seed), 14)
    log_vol = jnp.clip(-2.3 + 1.8 * jax.random.uniform(streams_of[0], (U, NE * NK), jnp.float32) ** levels(streams_of[0], (U, NE * NK), ((0, 8),), -0.2, 0.2), -2.3, -0.5)
    beta = jnp.clip(jnp.exp(math.log(2.0) - 1.3862944 * jax.random.uniform(streams_of[1], (U,), jnp.float32) ** levels(streams_of[1], (U,), ((0, 8),), -0.2, 0.2)), 0.5, 2.0)
    shock_table = jnp.clip(jax.random.uniform(streams_of[2], (NSHOCK, NE * NK), jnp.float32, -0.29882812, 0.3984375), -0.29882812, 0.3984375).astype(jnp.bfloat16)
    scen_ids = set_ends(jax.random.randint(streams_of[3], (SCEN,), 0, NSHOCK), jax.random.fold_in(streams_of[3], 1), 0, NSHOCK - 1).astype(jnp.int32)
    hot_index = set_ends(jax.random.randint(streams_of[4], (HOTS,), 0, U_DEV), jax.random.fold_in(streams_of[4], 1), 0, U_DEV - 1).astype(jnp.int32)
    dest_keys = jax.random.split(jax.random.fold_in(streams_of[5], 1), TRADES // TR_SUB)
    dest_turns = jax.random.permutation(jax.random.fold_in(streams_of[5], 3), TRADES // TR_SUB)
    dest = jax.vmap(lambda own, number: routed_block(jax.random.fold_in(streams_of[5], 2), own, number, TR_SUB, N_TRADE, 1, CAP, 2))(dest_keys, dest_turns).reshape((TRADES, 1))
    pick = set_ends(jax.random.randint(streams_of[6], (TRADES,), 0, HELD), jax.random.fold_in(streams_of[6], 1), 0, HELD - 1).astype(jnp.int32)
    expiry_cell = set_ends(jax.random.randint(streams_of[7], (TRADES,), 1, NE - 2), jax.random.fold_in(streams_of[7], 1), 1, (NE - 2) - 1).astype(jnp.int32)
    strike_cell = set_ends(jax.random.randint(streams_of[8], (TRADES,), 1, NK - 2), jax.random.fold_in(streams_of[8], 1), 1, (NK - 2) - 1).astype(jnp.int32)
    frac_e = jnp.clip(1.0 * jax.random.uniform(streams_of[9], (TRADES,), jnp.float32) ** levels(streams_of[9], (TRADES,), ((0, 8),), -0.2, 0.2), 0.0, 1.0)
    frac_k = jnp.clip(1.0 * jax.random.uniform(streams_of[10], (TRADES,), jnp.float32) ** levels(streams_of[10], (TRADES,), ((0, 8),), -0.2, 0.2), 0.0, 1.0)
    notional = normal_values(streams_of[11], (TRADES,), 3.0, 12.0, ((0, 8),), jnp.float32)
    forward = jnp.clip(jnp.exp(math.log(2.0) - 1.3862944 * jax.random.uniform(streams_of[12], (TRADES,), jnp.float32) ** levels(streams_of[12], (TRADES,), ((0, 8),), -0.2, 0.2)), 0.5, 2.0)
    return {"log_vol": log_vol, "beta": beta, "shock_table": shock_table, "scen_ids": scen_ids, "hot_index": hot_index, "dest": dest, "pick": pick, "expiry_cell": expiry_cell, "strike_cell": strike_cell, "frac_e": frac_e, "frac_k": frac_k, "notional": notional, "forward": forward}


RATE = 0.03
INV_ROOT_TWO = 0.7071067811865476
INV_ROOT_TAU = 0.3989422804014327

def spline_weights(offset):
    square = offset * offset
    offset_cube = square * offset
    return (0.5 * (2.0 * square - offset_cube - offset), 0.5 * (3.0 * offset_cube - 5.0 * square + 2.0), 0.5 * (4.0 * square - 3.0 * offset_cube + offset), 0.5 * (offset_cube - square))

def black_model(log_sigma, expiry_cell, frac_e, strike_cell, frac_k, notional, forward):
    maturity = (expiry_cell + frac_e + 1.0) * (4.0 / NE)
    moneyness = (strike_cell + frac_k - 0.5 * (NK - 1)) / NK
    root_time = jnp.sqrt(maturity)
    spread = jnp.exp(log_sigma) * root_time
    upper_d = -moneyness / spread + 0.5 * spread
    minus_term_black = upper_d - spread
    discount_factor = jnp.exp(-RATE * maturity)
    cdf_upper = 0.5 * lax.erfc(-upper_d * INV_ROOT_TWO)
    cdf_lower = 0.5 * lax.erfc(-minus_term_black * INV_ROOT_TWO)
    scaled = notional * discount_factor
    price_out = scaled * forward * (cdf_upper - jnp.exp(moneyness) * cdf_lower)
    vega_out = scaled * forward * INV_ROOT_TAU * jnp.exp(-0.5 * upper_d * upper_d) * root_time
    delta_out = scaled * cdf_upper
    return (price_out, vega_out, delta_out)

def reference(log_vol, beta, shock_table, scen_ids, hot_index, dest, pick, expiry_cell, strike_cell, frac_e, frac_k, notional, forward):
    target = dest[:, 0]
    lower_dev = (target + N_TRADE - 1) % N_TRADE
    upper_dev = (target + 1) % N_TRADE
    offset = pick - U_DEV
    lower_pick = jnp.clip(offset, 0, HOT - 1)
    upper_choice = jnp.clip(offset - HOT, 0, HOT - 1)
    from_lower = lower_dev * U_DEV + hot_index[lower_dev * HOT + lower_pick]
    from_upper = upper_dev * U_DEV + hot_index[upper_dev * HOT + upper_choice]
    underlying = jnp.where(pick < U_DEV, target * U_DEV + pick, jnp.where(offset < HOT, from_lower, from_upper)).astype(jnp.int32)
    weights_e = [lax.optimization_barrier(weight.astype(jnp.bfloat16)).astype(jnp.float32) for weight in spline_weights(frac_e)]
    strike_interp_coefs = spline_weights(frac_k)
    base_index = (underlying * (NE * NK) + (expiry_cell - 1) * NK + (strike_cell - 1)).astype(jnp.int32)
    shifts = shock_table[scen_ids].astype(jnp.float32)

    def one_scenario(shift_row):
        shocked = lax.optimization_barrier((log_vol + beta[:, None] * shift_row[None, :]).astype(jnp.bfloat16)).reshape(-1)
        accumulated = jnp.zeros(base_index.shape, jnp.float32)
        for second in range(4):
            inner_sum = jnp.zeros(base_index.shape, jnp.float32)
            for position in range(4):
                gathered = shocked[base_index + position * NK + second].astype(jnp.float32)
                inner_sum = inner_sum + weights_e[position] * gathered
            accumulated = accumulated + strike_interp_coefs[second] * inner_sum
        return accumulated
    log_sigma = lax.map(one_scenario, shifts)
    price_out, vega_out, delta_out = black_model(log_sigma, expiry_cell.astype(jnp.float32), frac_e, strike_cell.astype(jnp.float32), frac_k, notional, forward)
    return (price_out, vega_out, delta_out)
```

```python
import functools

import jax
import jax.numpy as jnp
from jax import lax
from jax.experimental import pallas as pl
from jax.experimental.pallas import tpu as pltpu
from jax.sharding import PartitionSpec as P

NE = 64
NK = 32
HOT = 2
LANES = 128
BAND = LANES // NK
BLOCKS = NE // BAND
EXTRA = 16
CENTRE = 1.4

RATE = 0.03
INV_ROOT_TWO = 0.7071067811865476
INV_ROOT_TAU = 0.3989422804014327

VMEM = pl.BlockSpec(memory_space=pltpu.VMEM)
SMEM = pl.BlockSpec(memory_space=pltpu.SMEM)
F32 = jnp.float32
BF16 = jnp.bfloat16

(WE, WK, ROW, COL, BLK, SLOT, PICK) = (0, 4, 8, 9, 10, 11, 12)
PREPARED = 13


def spline_weights(offset):
    square = offset * offset
    offset_cube = square * offset
    return (
        0.5 * (2.0 * square - offset_cube - offset),
        0.5 * (3.0 * offset_cube - 5.0 * square + 2.0),
        0.5 * (4.0 * square - 3.0 * offset_cube + offset),
        0.5 * (offset_cube - square),
    )


def params(megabytes=None):
    limit = None if megabytes is None else megabytes << 20
    return pltpu.CompilerParams(vmem_limit_bytes=limit)


def pack_kernel(hot_ref, log_vol_ref, beta_ref, out_ref):
    owned = log_vol_ref.shape[0]
    per_tile = LANES // owned
    for tile in range(BLOCKS // per_tile):
        stacked = jnp.concatenate(
            [
                log_vol_ref[:, (tile * per_tile + i) * LANES : (tile * per_tile + i + 1) * LANES]
                for i in range(per_tile)
            ],
            axis=0,
        )
        out_ref[0:LANES, tile * LANES : (tile + 1) * LANES] = (
            jnp.transpose(stacked) + CENTRE
        ).astype(BF16)
    row = lax.broadcasted_iota(jnp.int32, (EXTRA, LANES), 0)
    beta = jnp.broadcast_to(beta_ref[...], (EXTRA, LANES))
    high = beta.astype(BF16).astype(F32)
    middle = (beta - high).astype(BF16).astype(F32)
    low = beta - high - middle
    zero = jnp.zeros((EXTRA, LANES), F32)
    pieces = jnp.where(row == 0, high, jnp.where(row == 1, middle, jnp.where(row == 2, low, zero)))
    hots = zero
    for i in range(HOT):
        hots = jnp.where(row == i, hot_ref[i].astype(F32), hots)
    out_ref[LANES : LANES + EXTRA, 0:LANES] = pieces.astype(BF16)
    out_ref[LANES : LANES + EXTRA, LANES : 2 * LANES] = hots.astype(BF16)
    for tile in range(2, BLOCKS // per_tile):
        out_ref[LANES : LANES + EXTRA, tile * LANES : (tile + 1) * LANES] = zero.astype(BF16)


def placed(position, weights, first, shape):
    distance = position - jnp.broadcast_to(first, shape)
    result = jnp.zeros(shape, F32)
    for tap in range(4):
        result = jnp.where(distance == float(tap), jnp.broadcast_to(weights[tap], shape), result)
    return result


def prepare_kernel(
    device_count,
    per_step,
    place_ref,
    shift_ref,
    dest_ref,
    pick_ref,
    expiry_ref,
    strike_ref,
    frac_e_ref,
    frac_k_ref,
    out_ref,
    high_ref,
):
    groups = dest_ref.shape[0]
    owned = place_ref[2]
    n_scen = place_ref[3]
    weights = spline_weights(frac_e_ref[...])
    for tap in range(4):
        out_ref[WE + tap] = weights[tap].astype(BF16).astype(F32)
    weights = spline_weights(frac_k_ref[...])
    for tap in range(4):
        out_ref[WK + tap] = weights[tap]
    first_row = expiry_ref[...] - 1
    block = lax.shift_right_logical(first_row, BAND.bit_length() - 1)
    out_ref[ROW] = (first_row - block * BAND).astype(F32)
    out_ref[BLK] = block.astype(F32)
    out_ref[COL] = (strike_ref[...] - 1).astype(F32)
    dest = dest_ref[...]
    pick = pick_ref[...]
    hot = pick - owned
    step = jnp.where(hot < 0, 0, jnp.where(hot < HOT, device_count - 1, 1))
    owner = (dest + step) & (device_count - 1)
    offset = owner ^ place_ref[0]
    mine = (offset & (n_scen - 1)) == place_ref[1]
    slot = lax.shift_right_logical(offset, place_ref[4])
    out_ref[SLOT] = jnp.where(mine, slot, -1).astype(F32)
    out_ref[PICK] = jnp.where(hot < HOT, pick, pick - HOT).astype(F32)

    shift = shift_ref[...]
    scenarios = high_ref.shape[0]
    expiries = lax.broadcasted_iota(jnp.int32, (NE, LANES), 0).astype(F32)
    strikes = lax.broadcasted_iota(jnp.int32, (NK, LANES), 0).astype(F32)

    def some(i, carry):
        sides = []
        for part in range(per_step):
            g = i * per_step + part
            first = out_ref[BLK, pl.ds(g, 1), :] * float(BAND) + out_ref[ROW, pl.ds(g, 1), :]
            taps = [out_ref[WE + tap, pl.ds(g, 1), :] for tap in range(4)]
            sides.append(placed(expiries, taps, first, (NE, LANES)).astype(BF16))
        mixed = jnp.dot(shift, jnp.concatenate(sides, axis=1), preferred_element_type=F32)
        for part in range(per_step):
            g = i * per_step + part
            taps = [out_ref[WK + tap, pl.ds(g, 1), :] for tap in range(4)]
            coefs = placed(strikes, taps, out_ref[COL, pl.ds(g, 1), :], (NK, LANES))
            for s in range(scenarios):
                piece = mixed[s * NK : (s + 1) * NK, part * LANES : (part + 1) * LANES]
                high_ref[s, pl.ds(g, 1), :] = jnp.sum(piece * coefs, axis=0, keepdims=True)
        return carry

    lax.fori_loop(0, groups // per_step, some, 0)


def surface_kernel(slots, owned, per_step, *refs):
    messages = refs[:slots]
    pre_ref, out_ref, table_ref, index_ref = refs[slots:]
    groups = pre_ref.shape[1]
    depth = BLOCKS * owned
    for k in range(slots):
        here = messages[k][0:LANES, :]
        table_ref[k, 0:LANES, :] = here
        table_ref[k, LANES : 2 * LANES, :] = pltpu.roll(
            here.astype(F32), depth - owned, 1
        ).astype(BF16)
    sub = 8
    extras = [messages[k][LANES : LANES + EXTRA, 0 : 2 * LANES].astype(F32) for k in range(slots)]

    for i in range(groups // sub):
        rows = pl.ds(i * sub, sub)
        slot = pre_ref[SLOT, rows, :]
        pick = pre_ref[PICK, rows, :]
        index = jnp.full((sub, LANES), -1.0, F32)
        beta = jnp.zeros((sub, LANES), F32)
        for k in range(slots):
            local = pick
            for h in range(HOT):
                hot = jnp.broadcast_to(extras[k][h : h + 1, LANES : 2 * LANES], (sub, LANES))
                local = jnp.where(pick == float(owned + h), hot, local)
            row = extras[k][0:1, 0:LANES] + extras[k][1:2, 0:LANES] + extras[k][2:3, 0:LANES]
            looked = jnp.take_along_axis(
                jnp.broadcast_to(row, (sub, LANES)),
                local.astype(jnp.int32),
                axis=1,
                mode="promise_in_bounds",
            )
            index = jnp.where(slot == float(k), local + float(k * owned), index)
            beta = jnp.where(slot == float(k), looked, beta)
        index_ref[rows, :] = index
        out_ref[pl.ds(groups + i * sub, sub), :] = beta

    height = slots * owned
    underlyings = lax.broadcasted_iota(jnp.int32, (height, LANES), 0).astype(F32)
    strikes = lax.broadcasted_iota(jnp.int32, (NK, LANES), 0).astype(F32)
    expiries = lax.broadcasted_iota(jnp.int32, (2 * BAND, LANES), 0).astype(F32)

    def some(i, carry):
        chosen, block = [], []
        for part in range(per_step):
            g = i * per_step + part
            index = jnp.broadcast_to(index_ref[pl.ds(g, 1), :], (height, LANES))
            chosen.append(jnp.where(underlyings == index, 1.0, 0.0).astype(BF16))
            block.append(
                jnp.broadcast_to(pre_ref[BLK, pl.ds(g, 1), :], (owned, LANES)).astype(BF16)
            )
        total = None
        zero = jnp.zeros((owned, LANES), BF16)
        for k in range(slots):
            side = jnp.concatenate(
                [
                    jnp.concatenate(
                        [
                            jnp.where(
                                block[part] == jnp.asarray(j, BF16),
                                chosen[part][k * owned : (k + 1) * owned],
                                zero,
                            )
                            for j in range(BLOCKS)
                        ],
                        axis=0,
                    )
                    for part in range(per_step)
                ],
                axis=1,
            )
            product = jnp.dot(table_ref[k], side, preferred_element_type=F32)
            total = product if total is None else total + product
        for part in range(per_step):
            g = i * per_step + part
            columns = slice(part * LANES, (part + 1) * LANES)
            taps = [pre_ref[WE + tap, pl.ds(g, 1), :] for tap in range(4)]
            mix = placed(expiries, taps, pre_ref[ROW, pl.ds(g, 1), :], (2 * BAND, LANES))
            curve = jnp.zeros((NK, LANES), F32)
            for a in range(2 * BAND):
                curve = curve + total[a * NK : (a + 1) * NK, columns] * mix[a : a + 1, :]
            taps = [pre_ref[WK + tap, pl.ds(g, 1), :] for tap in range(4)]
            coefs = placed(strikes, taps, pre_ref[COL, pl.ds(g, 1), :], (NK, LANES))
            level = jnp.sum(curve * coefs, axis=0, keepdims=True)
            weight = (taps[0] + taps[1] + taps[2] + taps[3]) * jnp.sum(mix, axis=0, keepdims=True)
            held = index_ref[pl.ds(g, 1), :] >= 0.0
            out_ref[pl.ds(g, 1), :] = jnp.where(held, level - CENTRE * weight, 0.0)
        return carry

    lax.fori_loop(0, groups // per_step, some, 0)


def black_model(log_sigma, expiry_cell, frac_e, strike_cell, frac_k, notional, forward):
    maturity = (expiry_cell + frac_e + 1.0) * (4.0 / NE)
    moneyness = (strike_cell + frac_k - 0.5 * (NK - 1)) / NK
    root_time = jnp.sqrt(maturity)
    spread = jnp.exp(log_sigma) * root_time
    upper_d = -moneyness / spread + 0.5 * spread
    minus_term_black = upper_d - spread
    discount_factor = jnp.exp(-RATE * maturity)
    cdf_upper = 0.5 * lax.erfc(-upper_d * INV_ROOT_TWO)
    cdf_lower = 0.5 * lax.erfc(-minus_term_black * INV_ROOT_TWO)
    scaled = notional * discount_factor
    price_out = scaled * forward * (cdf_upper - jnp.exp(moneyness) * cdf_lower)
    vega_out = scaled * forward * INV_ROOT_TAU * jnp.exp(-0.5 * upper_d * upper_d) * root_time
    delta_out = scaled * cdf_upper
    return (price_out, vega_out, delta_out)


def shards(
    log_vol,
    beta,
    shock_table,
    scen_ids,
    hot_index,
    dest,
    pick,
    expiry_cell,
    strike_cell,
    frac_e,
    frac_k,
    notional,
    forward,
):
    n_trade = lax.axis_size("trade")
    n_scen = lax.axis_size("scen")
    slots = n_trade // n_scen
    owned = log_vol.shape[0]
    trades = pick.shape[0]
    groups = trades // LANES
    scenarios = scen_ids.shape[0]

    beta_row = jnp.pad(beta[None, :], ((0, 0), (0, LANES - owned)))
    message = pl.pallas_call(
        pack_kernel,
        out_shape=jax.ShapeDtypeStruct((LANES + EXTRA, BLOCKS * owned), BF16),
        in_specs=[SMEM, VMEM, VMEM],
        out_specs=VMEM,
        compiler_params=params(),
    )(hot_index, log_vol, beta_row)

    received = [None] * slots
    for k in reversed(range(slots)):
        pairs = [
            ((d ^ (q + k * n_scen)) * n_scen + q, d * n_scen + q)
            for d in range(n_trade)
            for q in range(n_scen)
        ]
        received[k] = lax.ppermute(message, ("trade", "scen"), pairs)

    shift = jnp.concatenate(
        [
            lax.dynamic_slice(shock_table, (scen_ids[s], 0), (1, NE * NK))
            for s in range(scenarios)
        ],
        axis=0,
    )
    shift = shift.reshape(scenarios, NE, NK).transpose(0, 2, 1).reshape(scenarios * NK, NE)
    dense = [
        column.reshape(groups, LANES)
        for column in (dest, pick, expiry_cell, strike_cell, frac_e, frac_k)
    ]
    place = jnp.stack(
        [
            lax.axis_index("trade"),
            lax.axis_index("scen"),
            jnp.int32(owned),
            jnp.int32(n_scen),
            jnp.int32(n_scen.bit_length() - 1),
        ]
    )
    prepared, shift_level = pl.pallas_call(
        functools.partial(prepare_kernel, n_trade, 4),
        out_shape=(
            jax.ShapeDtypeStruct((PREPARED, groups, LANES), F32),
            jax.ShapeDtypeStruct((scenarios, groups, LANES), F32),
        ),
        in_specs=[SMEM] + [VMEM] * 7,
        out_specs=(VMEM, VMEM),
        cost_estimate=pl.CostEstimate(flops=40_000_000, bytes_accessed=6_000_000, transcendentals=0),
        compiler_params=params(),
    )(place, shift, *dense)

    partial_levels = pl.pallas_call(
        functools.partial(surface_kernel, slots, owned, 4),
        out_shape=jax.ShapeDtypeStruct((2 * groups, LANES), F32),
        in_specs=[VMEM] * (slots + 1),
        out_specs=VMEM,
        scratch_shapes=[
            pltpu.VMEM((slots, 2 * LANES, BLOCKS * owned), BF16),
            pltpu.VMEM((groups, LANES), F32),
        ],
        compiler_params=params(48),
    )(*received, prepared)

    total = partial_levels
    hop = n_scen // 2
    while hop:
        total = total + lax.ppermute(total, "scen", [(i, i ^ hop) for i in range(n_scen)])
        hop //= 2
    level = total[:groups].reshape(trades)
    slope = total[groups:].reshape(trades)
    log_sigma = level[None, :] + slope[None, :] * shift_level.reshape(scenarios, trades)
    return black_model(
        log_sigma,
        expiry_cell.astype(F32),
        frac_e,
        strike_cell.astype(F32),
        frac_k,
        notional,
        forward,
    )


def solution(mesh):
    in_specs = (
        P("trade", None),
        P("trade"),
        P(),
        P("scen"),
        P("trade"),
        P("trade", None),
        P("trade"),
        P("trade"),
        P("trade"),
        P("trade"),
        P("trade"),
        P("trade"),
        P("trade"),
    )
    out_specs = (P("scen", "trade"), P("scen", "trade"), P("scen", "trade"))
    return jax.shard_map(shards, mesh=mesh, in_specs=in_specs, out_specs=out_specs, check_vma=False)
```

```python
import functools

import jax
import jax.numpy as jnp
from jax import lax
from jax.experimental import pallas as pl
from jax.experimental.pallas import tpu as pltpu
from jax.sharding import PartitionSpec as P

NE = 64
NK = 32
HOT = 2
LANES = 128
BAND = 8
BLOCKS = NE // BAND
TILES = BAND * NK // LANES
WIDE = BAND * NK
REACH = BAND + 3
EXTRA = 16
CENTRE = 1.4
PREPARE_STEP = 16
SURFACE_STEP = 16

RATE = 0.03
INV_ROOT_TWO = 0.7071067811865476
INV_ROOT_TAU = 0.3989422804014327

VMEM = pl.BlockSpec(memory_space=pltpu.VMEM)
HBM = pl.BlockSpec(memory_space=pltpu.HBM)
F32 = jnp.float32
BF16 = jnp.bfloat16

(WE, WK, ROW, COL, BLK, SLOT, PICK) = (0, 4, 8, 9, 10, 11, 12)
(ROOT, MONEY, GROWTH, CASH, VALUE) = (13, 14, 15, 16, 17)
PREPARED = 18


def spline_weights(offset):
    square = offset * offset
    offset_cube = square * offset
    return (
        0.5 * (2.0 * square - offset_cube - offset),
        0.5 * (3.0 * offset_cube - 5.0 * square + 2.0),
        0.5 * (4.0 * square - 3.0 * offset_cube + offset),
        0.5 * (offset_cube - square),
    )


def params(kilobytes):
    return pltpu.CompilerParams(vmem_limit_bytes=kilobytes << 10)


def pack_kernel(hot_in, log_vol_in, beta_in, out_ref, log_vol_ref, beta_ref, hot_ref, sems, small):
    owned = log_vol_ref.shape[0]
    per_tile = LANES // owned
    steps = BLOCKS // per_tile
    width = log_vol_ref.shape[1] // steps
    copies = []
    for tile in range(steps):
        columns = pl.ds(tile * width, width)
        copies.append(
            pltpu.make_async_copy(
                log_vol_in.at[:, columns], log_vol_ref.at[:, columns], sems.at[tile]
            )
        )
    copies.append(pltpu.make_async_copy(beta_in, beta_ref, small.at[0]))
    copies.append(pltpu.make_async_copy(hot_in, hot_ref, small.at[1]))
    for copy in copies:
        copy.start()
    for tile in range(steps):
        copies[tile].wait()
        for half in range(TILES):
            first = [((tile * per_tile + i) * TILES + half) * LANES for i in range(per_tile)]
            stacked = jnp.concatenate([log_vol_ref[:, c : c + LANES] for c in first], axis=0)
            out_ref[half * LANES : (half + 1) * LANES, tile * LANES : (tile + 1) * LANES] = (
                jnp.transpose(stacked) + CENTRE
            ).astype(BF16)
    copies[steps].wait()
    copies[steps + 1].wait()
    row = lax.broadcasted_iota(jnp.int32, (EXTRA, LANES), 0)
    beta = jnp.broadcast_to(beta_ref[...], (EXTRA, owned))
    high = beta.astype(BF16).astype(F32)
    middle = (beta - high).astype(BF16).astype(F32)
    low = beta - high - middle
    zero = jnp.zeros((EXTRA, LANES), F32)
    row_b = row[:, 0:owned]
    pieces = jnp.where(row_b == 0, high, jnp.where(row_b == 1, middle, jnp.where(row_b == 2, low, 0.0)))
    hots = zero
    for i in range(HOT):
        hots = jnp.where(row == i, hot_ref[i].astype(F32), hots)
    out_ref[WIDE : WIDE + EXTRA, 0:LANES] = zero.astype(BF16)
    out_ref[WIDE : WIDE + EXTRA, 0:owned] = pieces.astype(BF16)
    out_ref[WIDE : WIDE + EXTRA, LANES : 2 * LANES] = hots.astype(BF16)
    for tile in range(2, BLOCKS // per_tile):
        out_ref[WIDE : WIDE + EXTRA, tile * LANES : (tile + 1) * LANES] = zero.astype(BF16)


def placed(position, weights, first, shape):
    distance = position - jnp.broadcast_to(first, shape)
    result = jnp.zeros(shape, F32)
    for tap in range(4):
        result = jnp.where(distance == float(tap), jnp.broadcast_to(weights[tap], shape), result)
    return result


def prepare_kernel(
    device_count,
    n_scen,
    owned,
    per_step,
    scen_in,
    shock_ref,
    *refs,
):
    whole, reals = refs[:4], refs[4:8]
    out_ref, shift_ref, scen_ref, whole_ref, real_ref, rows_ref, matrix_ref, sems, sem = refs[8:]
    groups = out_ref.shape[1]
    scenarios = shift_ref.shape[0]
    ids = pltpu.make_async_copy(scen_in, scen_ref, sems.at[8])
    ids.start()
    columns = []
    for i in range(4):
        columns.append(pltpu.make_async_copy(whole[i], whole_ref.at[i], sems.at[i]))
        columns.append(pltpu.make_async_copy(reals[i], real_ref.at[i], sems.at[4 + i]))
    for copy in columns:
        copy.start()
    ids.wait()
    copies = []
    for s in range(scenarios):
        first = pl.multiple_of(lax.shift_right_logical(scen_ref[s], 4) * 16, 16)
        copies.append(
            pltpu.make_async_copy(shock_ref.at[pl.ds(first, 16), :], rows_ref.at[s], sem.at[s])
        )
        copies[-1].start()
    for copy in columns:
        copy.wait()
    dest, pick, expiry, strike = [whole_ref[i] for i in range(4)]
    frac_e, frac_k, notional, forward = [real_ref[i] for i in range(4)]
    weights = spline_weights(frac_e)
    for tap in range(4):
        out_ref[WE + tap] = weights[tap].astype(BF16).astype(F32)
    weights = spline_weights(frac_k)
    for tap in range(4):
        out_ref[WK + tap] = weights[tap]
    first_row = expiry - 1
    block = lax.shift_right_logical(first_row, BAND.bit_length() - 1)
    out_ref[ROW] = (first_row - block * BAND).astype(F32)
    out_ref[BLK] = block.astype(F32)
    out_ref[COL] = (strike - 1).astype(F32)
    hot = pick - owned
    step = jnp.where(hot < 0, 0, jnp.where(hot < HOT, device_count - 1, 1))
    owner = (dest + step) & (device_count - 1)
    offset = owner ^ lax.axis_index("trade")
    mine = (offset & (n_scen - 1)) == lax.axis_index("scen")
    slot = lax.shift_right_logical(offset, n_scen.bit_length() - 1)
    out_ref[SLOT] = jnp.where(mine, slot, -1).astype(F32)
    out_ref[PICK] = jnp.where(hot < HOT, pick, pick - HOT).astype(F32)

    maturity = (expiry.astype(F32) + frac_e + 1.0) * (4.0 / NE)
    moneyness = (strike.astype(F32) + frac_k - 0.5 * (NK - 1)) / NK
    scaled = notional * jnp.exp(-RATE * maturity)
    out_ref[ROOT] = jnp.sqrt(maturity)
    out_ref[MONEY] = moneyness
    out_ref[GROWTH] = jnp.exp(moneyness)
    out_ref[CASH] = scaled
    out_ref[VALUE] = scaled * forward

    tiles = NE * NK // LANES
    in_tile = LANES // NK
    line = lax.broadcasted_iota(jnp.int32, (16, NE * NK), 0)
    for s in range(scenarios):
        copies[s].wait()
        wanted = jnp.where(line == (scen_ref[s] & 15), rows_ref[s].astype(F32), 0.0)
        wanted = jnp.sum(wanted, axis=0, keepdims=True)
        stacked = jnp.concatenate(
            [wanted[:, i * LANES : (i + 1) * LANES] for i in range(tiles)], axis=0
        )
        turned = jnp.transpose(stacked)
        for i in range(in_tile):
            matrix_ref[s * NK : (s + 1) * NK, i * tiles : (i + 1) * tiles] = turned[
                i * NK : (i + 1) * NK, :
            ]
    shift = matrix_ref[...].astype(BF16)
    place = lax.broadcasted_iota(jnp.int32, (NE, LANES), 0)
    expiries = (
        (place & (tiles - 1)) * in_tile + lax.shift_right_logical(place, tiles.bit_length() - 1)
    ).astype(F32)
    strikes = lax.broadcasted_iota(jnp.int32, (NK, LANES), 0).astype(F32)

    def some(i, carry):
        sides = []
        for part in range(per_step):
            g = i * per_step + part
            first = out_ref[BLK, pl.ds(g, 1), :] * float(BAND) + out_ref[ROW, pl.ds(g, 1), :]
            taps = [out_ref[WE + tap, pl.ds(g, 1), :] for tap in range(4)]
            sides.append(placed(expiries, taps, first, (NE, LANES)).astype(BF16))
        mixed = jnp.dot(shift, jnp.concatenate(sides, axis=1), preferred_element_type=F32)
        for part in range(per_step):
            g = i * per_step + part
            taps = [out_ref[WK + tap, pl.ds(g, 1), :] for tap in range(4)]
            coefs = placed(strikes, taps, out_ref[COL, pl.ds(g, 1), :], (NK, LANES))
            for s in range(scenarios):
                piece = mixed[s * NK : (s + 1) * NK, part * LANES : (part + 1) * LANES]
                shift_ref[s, pl.ds(g, 1), :] = jnp.sum(piece * coefs, axis=0, keepdims=True)
        return carry

    lax.fori_loop(0, groups // per_step, some, 0)


def surface_kernel(slot, owned, per_step, message_ref, pre_ref, *refs):
    before_ref = refs[0] if len(refs) == 4 else None
    out_ref, table_ref, index_ref = refs[-3:]
    groups = pre_ref.shape[1]
    table_ref[0:WIDE, :] = message_ref[0:WIDE, :]
    table_ref[WIDE : WIDE + 3 * NK, :] = pltpu.roll(
        message_ref[0 : 3 * NK, :].astype(F32), (BLOCKS - 1) * owned, 1
    ).astype(BF16)
    extra = message_ref[WIDE : WIDE + EXTRA, 0 : 2 * LANES].astype(F32)
    betas = extra[0:1, 0:LANES] + extra[1:2, 0:LANES] + extra[2:3, 0:LANES]
    sub = 8
    for i in range(groups // sub):
        rows = pl.ds(i * sub, sub)
        held = pre_ref[SLOT, rows, :] == float(slot)
        local = pre_ref[PICK, rows, :]
        for h in range(HOT):
            hot = jnp.broadcast_to(extra[h : h + 1, LANES : 2 * LANES], (sub, LANES))
            local = jnp.where(local == float(owned + h), hot, local)
        looked = jnp.take_along_axis(
            jnp.broadcast_to(betas, (sub, LANES)),
            local.astype(jnp.int32),
            axis=1,
            mode="promise_in_bounds",
        )
        index_ref[rows, :] = jnp.where(held, local, -1.0)
        later = pl.ds(groups + i * sub, sub)
        other = 0.0 if before_ref is None else before_ref[later, :]
        out_ref[later, :] = jnp.where(held, looked, other)

    underlyings = lax.broadcasted_iota(jnp.int32, (owned, LANES), 0).astype(F32)
    strikes = lax.broadcasted_iota(jnp.int32, (NK, LANES), 0).astype(F32)
    expiries = lax.broadcasted_iota(jnp.int32, (2 * BAND, LANES), 0).astype(F32)
    zero = jnp.zeros((owned, LANES), BF16)

    def some(i, carry):
        sides = []
        for part in range(per_step):
            g = i * per_step + part
            index = jnp.broadcast_to(index_ref[pl.ds(g, 1), :], (owned, LANES))
            chosen = jnp.where(underlyings == index, 1.0, 0.0).astype(BF16)
            block = jnp.broadcast_to(pre_ref[BLK, pl.ds(g, 1), :], (owned, LANES)).astype(BF16)
            sides.append(
                jnp.concatenate(
                    [
                        jnp.where(block == jnp.asarray(j, BF16), chosen, zero)
                        for j in range(BLOCKS)
                    ],
                    axis=0,
                )
            )
        product = jnp.dot(
            table_ref[...], jnp.concatenate(sides, axis=1), preferred_element_type=F32
        )
        for part in range(per_step):
            g = i * per_step + part
            columns = slice(part * LANES, (part + 1) * LANES)
            taps = [pre_ref[WE + tap, pl.ds(g, 1), :] for tap in range(4)]
            mix = placed(expiries, taps, pre_ref[ROW, pl.ds(g, 1), :], (2 * BAND, LANES))
            curve = jnp.zeros((NK, LANES), F32)
            for a in range(REACH):
                curve = curve + product[a * NK : (a + 1) * NK, columns] * mix[a : a + 1, :]
            taps_k = [pre_ref[WK + tap, pl.ds(g, 1), :] for tap in range(4)]
            coefs = placed(strikes, taps_k, pre_ref[COL, pl.ds(g, 1), :], (NK, LANES))
            level = jnp.sum(curve * coefs, axis=0, keepdims=True)
            weight = (taps[0] + taps[1] + taps[2] + taps[3]) * (
                taps_k[0] + taps_k[1] + taps_k[2] + taps_k[3]
            )
            held = index_ref[pl.ds(g, 1), :] >= 0.0
            other = 0.0 if before_ref is None else before_ref[pl.ds(g, 1), :]
            out_ref[pl.ds(g, 1), :] = jnp.where(held, level - CENTRE * weight, other)
        return carry

    lax.fori_loop(0, groups // per_step, some, 0)


def value_kernel(part_ref, rest_ref, shift_ref, pre_ref, price_ref, vega_ref, delta_ref):
    scenarios, groups = shift_ref.shape[0], shift_ref.shape[1]
    sub = 8
    for i in range(groups // sub):
        rows = pl.ds(i * sub, sub)
        later = pl.ds(groups + i * sub, sub)
        level = part_ref[rows, :] + rest_ref[rows, :]
        slope = part_ref[later, :] + rest_ref[later, :]
        root_time = pre_ref[ROOT, rows, :]
        moneyness = pre_ref[MONEY, rows, :]
        growth = pre_ref[GROWTH, rows, :]
        scaled = pre_ref[CASH, rows, :]
        value = pre_ref[VALUE, rows, :]
        results = ([], [], [])
        for s in range(scenarios):
            spread = jnp.exp(level + slope * shift_ref[s, rows, :]) * root_time
            upper_d = -moneyness / spread + 0.5 * spread
            lower_d = upper_d - spread
            cdf_upper = 0.5 + 0.5 * lax.erf(upper_d * INV_ROOT_TWO)
            cdf_lower = 0.5 + 0.5 * lax.erf(lower_d * INV_ROOT_TWO)
            results[0].append(value * (cdf_upper - growth * cdf_lower))
            results[1].append(value * INV_ROOT_TAU * jnp.exp(-0.5 * upper_d * upper_d) * root_time)
            results[2].append(scaled * cdf_upper)
        for r in range(sub):
            columns = pl.ds((i * sub + r) * LANES, LANES)
            for ref, result in zip((price_ref, vega_ref, delta_ref), results):
                ref[:, columns] = jnp.concatenate([x[r : r + 1, :] for x in result], axis=0)


def shards(
    log_vol,
    beta,
    shock_table,
    scen_ids,
    hot_index,
    dest,
    pick,
    expiry_cell,
    strike_cell,
    frac_e,
    frac_k,
    notional,
    forward,
):
    n_trade = lax.axis_size("trade")
    n_scen = lax.axis_size("scen")
    slots = n_trade // n_scen
    owned = log_vol.shape[0]
    trades = pick.shape[0]
    groups = trades // LANES
    scenarios = scen_ids.shape[0]

    message = pl.pallas_call(
        pack_kernel,
        out_shape=jax.ShapeDtypeStruct((WIDE + EXTRA, BLOCKS * owned), BF16),
        in_specs=[HBM] * 3,
        out_specs=VMEM,
        scratch_shapes=[
            pltpu.VMEM(log_vol.shape, F32),
            pltpu.VMEM((1, owned), F32),
            pltpu.SMEM(hot_index.shape, jnp.int32),
            pltpu.SemaphoreType.DMA((BLOCKS * owned // LANES,)),
            pltpu.SemaphoreType.DMA((2,)),
        ],
        compiler_params=params(60000),
    )(hot_index, log_vol, beta.reshape(1, owned))

    received = [None] * slots
    for k in reversed(range(slots)):
        pairs = [
            ((d ^ (q + k * n_scen)) * n_scen + q, d * n_scen + q)
            for d in range(n_trade)
            for q in range(n_scen)
        ]
        received[k] = lax.ppermute(message, ("trade", "scen"), pairs)

    dense = [
        column.reshape(groups, LANES)
        for column in (
            dest,
            pick,
            expiry_cell,
            strike_cell,
            frac_e,
            frac_k,
            notional,
            forward,
        )
    ]
    prepared, shift_level = pl.pallas_call(
        functools.partial(prepare_kernel, n_trade, n_scen, owned, PREPARE_STEP),
        out_shape=(
            jax.ShapeDtypeStruct((PREPARED, groups, LANES), F32),
            jax.ShapeDtypeStruct((scenarios, groups, LANES), F32),
        ),
        in_specs=[HBM] * 10,
        out_specs=(VMEM, VMEM),
        scratch_shapes=[
            pltpu.SMEM(scen_ids.shape, jnp.int32),
            pltpu.VMEM((4, groups, LANES), jnp.int32),
            pltpu.VMEM((4, groups, LANES), F32),
            pltpu.VMEM((scenarios, 16, NE * NK), BF16),
            pltpu.VMEM((scenarios * NK, NE), F32),
            pltpu.SemaphoreType.DMA((9,)),
            pltpu.SemaphoreType.DMA((scenarios,)),
        ],
        cost_estimate=pl.CostEstimate(flops=40_000_000, bytes_accessed=6_000_000, transcendentals=0),
        compiler_params=params(60000),
    )(scen_ids, shock_table, *dense)

    partial_levels = None
    for k in range(slots):
        before = [] if partial_levels is None else [partial_levels]
        partial_levels = pl.pallas_call(
            functools.partial(surface_kernel, k, owned, SURFACE_STEP),
            out_shape=jax.ShapeDtypeStruct((2 * groups, LANES), F32),
            in_specs=[VMEM] * (2 + len(before)),
            out_specs=VMEM,
            scratch_shapes=[
                pltpu.VMEM((WIDE + 3 * NK, BLOCKS * owned), BF16),
                pltpu.VMEM((groups, LANES), F32),
            ],
            compiler_params=params(24576),
        )(received[k], prepared, *before)

    rest = jnp.zeros_like(partial_levels) if n_scen == 1 else None
    hop = n_scen // 2
    while hop:
        if rest is not None:
            partial_levels = partial_levels + rest
        rest = lax.ppermute(partial_levels, "scen", [(i, i ^ hop) for i in range(n_scen)])
        hop //= 2
    return pl.pallas_call(
        value_kernel,
        out_shape=(jax.ShapeDtypeStruct((scenarios, trades), F32),) * 3,
        in_specs=[VMEM] * 4,
        out_specs=(VMEM,) * 3,
        compiler_params=params(8192),
    )(partial_levels, rest, shift_level, prepared)


def solution(mesh):
    in_specs = (
        P("trade", None),
        P("trade"),
        P(),
        P("scen"),
        P("trade"),
        P("trade", None),
        P("trade"),
        P("trade"),
        P("trade"),
        P("trade"),
        P("trade"),
        P("trade"),
        P("trade"),
    )
    out_specs = (P("scen", "trade"), P("scen", "trade"), P("scen", "trade"))
    return jax.shard_map(shards, mesh=mesh, in_specs=in_specs, out_specs=out_specs, check_vma=False)
```

```python
import functools

import jax
import jax.numpy as jnp
from jax import lax
from jax.experimental import pallas as pl
from jax.experimental.pallas import tpu as pltpu
from jax.sharding import PartitionSpec as P

NE = 64
NK = 32
HOT = 2
LANES = 128
BAND = 8
BLOCKS = NE // BAND
TILES = BAND * NK // LANES
WIDE = BAND * NK
REACH = BAND + 3
EXTRA = 16
CENTRE = 1.4
PREPARE_STEP = 16
SURFACE_STEP = 16

RATE = 0.03
INV_ROOT_TWO = 0.7071067811865476
INV_ROOT_TAU = 0.3989422804014327

VMEM = pl.BlockSpec(memory_space=pltpu.VMEM)
HBM = pl.BlockSpec(memory_space=pltpu.HBM)
F32 = jnp.float32
BF16 = jnp.bfloat16

(WE, WK, ROW, COL, BLK, SLOT, PICK) = (0, 4, 8, 9, 10, 11, 12)
(ROOT, MONEY, GROWTH, CASH, VALUE) = (13, 14, 15, 16, 17)
PREPARED = 18


def spline_weights(offset):
    square = offset * offset
    offset_cube = square * offset
    return (
        0.5 * (2.0 * square - offset_cube - offset),
        0.5 * (3.0 * offset_cube - 5.0 * square + 2.0),
        0.5 * (4.0 * square - 3.0 * offset_cube + offset),
        0.5 * (offset_cube - square),
    )


def in_hbm(*arrays):
    return [pltpu.with_memory_space_constraint(x, pltpu.HBM) if x.size > 1 else x for x in arrays]


def params(kilobytes):
    return pltpu.CompilerParams(vmem_limit_bytes=kilobytes << 10)


def pack_kernel(hot_in, log_vol_in, beta_in, out_ref, log_vol_ref, beta_ref, hot_ref, sems, small):
    owned = log_vol_ref.shape[0]
    per_tile = LANES // owned
    steps = BLOCKS // per_tile
    width = log_vol_ref.shape[1] // steps
    copies = []
    for tile in range(steps):
        columns = pl.ds(tile * width, width)
        copies.append(
            pltpu.make_async_copy(
                log_vol_in.at[:, columns], log_vol_ref.at[:, columns], sems.at[tile]
            )
        )
    copies.append(pltpu.make_async_copy(beta_in, beta_ref, small.at[0]))
    copies.append(pltpu.make_async_copy(hot_in, hot_ref, small.at[1]))
    for copy in copies:
        copy.start()
    for tile in range(steps):
        copies[tile].wait()
        for half in range(TILES):
            first = [((tile * per_tile + i) * TILES + half) * LANES for i in range(per_tile)]
            stacked = jnp.concatenate([log_vol_ref[:, c : c + LANES] for c in first], axis=0)
            out_ref[half * LANES : (half + 1) * LANES, tile * LANES : (tile + 1) * LANES] = (
                jnp.transpose(stacked) + CENTRE
            ).astype(BF16)
    copies[steps].wait()
    copies[steps + 1].wait()
    row = lax.broadcasted_iota(jnp.int32, (EXTRA, LANES), 0)
    beta = jnp.broadcast_to(beta_ref[...], (EXTRA, owned))
    high = beta.astype(BF16).astype(F32)
    middle = (beta - high).astype(BF16).astype(F32)
    low = beta - high - middle
    zero = jnp.zeros((EXTRA, LANES), F32)
    row_b = row[:, 0:owned]
    pieces = jnp.where(row_b == 0, high, jnp.where(row_b == 1, middle, jnp.where(row_b == 2, low, 0.0)))
    hots = zero
    for i in range(HOT):
        hots = jnp.where(row == i, hot_ref[i].astype(F32), hots)
    out_ref[WIDE : WIDE + EXTRA, 0:LANES] = zero.astype(BF16)
    out_ref[WIDE : WIDE + EXTRA, 0:owned] = pieces.astype(BF16)
    out_ref[WIDE : WIDE + EXTRA, LANES : 2 * LANES] = hots.astype(BF16)
    for tile in range(2, BLOCKS // per_tile):
        out_ref[WIDE : WIDE + EXTRA, tile * LANES : (tile + 1) * LANES] = zero.astype(BF16)


def placed(position, weights, first, shape):
    distance = position - jnp.broadcast_to(first, shape)
    result = jnp.zeros(shape, F32)
    for tap in range(4):
        result = jnp.where(distance == float(tap), jnp.broadcast_to(weights[tap], shape), result)
    return result


def prepare_kernel(
    device_count,
    n_scen,
    owned,
    per_step,
    scen_in,
    shock_ref,
    *refs,
):
    whole, reals = refs[:4], refs[4:8]
    out_ref, shift_ref, scen_ref, whole_ref, real_ref, rows_ref, matrix_ref, sems, sem = refs[8:]
    groups = out_ref.shape[1]
    scenarios = shift_ref.shape[0]
    ids = pltpu.make_async_copy(scen_in, scen_ref, sems.at[8])
    ids.start()
    columns = []
    for i in range(4):
        columns.append(pltpu.make_async_copy(whole[i], whole_ref.at[i], sems.at[i]))
        columns.append(pltpu.make_async_copy(reals[i], real_ref.at[i], sems.at[4 + i]))
    for copy in columns:
        copy.start()
    ids.wait()
    copies = []
    for s in range(scenarios):
        first = pl.multiple_of(lax.shift_right_logical(scen_ref[s], 4) * 16, 16)
        copies.append(
            pltpu.make_async_copy(shock_ref.at[pl.ds(first, 16), :], rows_ref.at[s], sem.at[s])
        )
        copies[-1].start()
    for copy in columns:
        copy.wait()
    dest, pick, expiry, strike = [whole_ref[i] for i in range(4)]
    frac_e, frac_k, notional, forward = [real_ref[i] for i in range(4)]
    weights = spline_weights(frac_e)
    for tap in range(4):
        out_ref[WE + tap] = weights[tap].astype(BF16).astype(F32)
    weights = spline_weights(frac_k)
    for tap in range(4):
        out_ref[WK + tap] = weights[tap]
    first_row = expiry - 1
    block = lax.shift_right_logical(first_row, BAND.bit_length() - 1)
    out_ref[ROW] = (first_row - block * BAND).astype(F32)
    out_ref[BLK] = block.astype(F32)
    out_ref[COL] = (strike - 1).astype(F32)
    hot = pick - owned
    step = jnp.where(hot < 0, 0, jnp.where(hot < HOT, device_count - 1, 1))
    owner = (dest + step) & (device_count - 1)
    offset = owner ^ lax.axis_index("trade")
    mine = (offset & (n_scen - 1)) == lax.axis_index("scen")
    slot = lax.shift_right_logical(offset, n_scen.bit_length() - 1)
    out_ref[SLOT] = jnp.where(mine, slot, -1).astype(F32)
    out_ref[PICK] = jnp.where(hot < HOT, pick, pick - HOT).astype(F32)

    maturity = (expiry.astype(F32) + frac_e + 1.0) * (4.0 / NE)
    moneyness = (strike.astype(F32) + frac_k - 0.5 * (NK - 1)) / NK
    scaled = notional * jnp.exp(-RATE * maturity)
    out_ref[ROOT] = jnp.sqrt(maturity)
    out_ref[MONEY] = moneyness
    out_ref[GROWTH] = jnp.exp(moneyness)
    out_ref[CASH] = scaled
    out_ref[VALUE] = scaled * forward

    tiles = NE * NK // LANES
    in_tile = LANES // NK
    line = lax.broadcasted_iota(jnp.int32, (16, NE * NK), 0)
    for s in range(scenarios):
        copies[s].wait()
        wanted = jnp.where(line == (scen_ref[s] & 15), rows_ref[s].astype(F32), 0.0)
        wanted = jnp.sum(wanted, axis=0, keepdims=True)
        stacked = jnp.concatenate(
            [wanted[:, i * LANES : (i + 1) * LANES] for i in range(tiles)], axis=0
        )
        turned = jnp.transpose(stacked)
        for i in range(in_tile):
            matrix_ref[s * NK : (s + 1) * NK, i * tiles : (i + 1) * tiles] = turned[
                i * NK : (i + 1) * NK, :
            ]
    shift = matrix_ref[...].astype(BF16)
    place = lax.broadcasted_iota(jnp.int32, (NE, LANES), 0)
    expiries = (
        (place & (tiles - 1)) * in_tile + lax.shift_right_logical(place, tiles.bit_length() - 1)
    ).astype(F32)
    strikes = lax.broadcasted_iota(jnp.int32, (NK, LANES), 0).astype(F32)

    def some(i, carry):
        sides = []
        for part in range(per_step):
            g = i * per_step + part
            first = out_ref[BLK, pl.ds(g, 1), :] * float(BAND) + out_ref[ROW, pl.ds(g, 1), :]
            taps = [out_ref[WE + tap, pl.ds(g, 1), :] for tap in range(4)]
            sides.append(placed(expiries, taps, first, (NE, LANES)).astype(BF16))
        mixed = jnp.dot(shift, jnp.concatenate(sides, axis=1), preferred_element_type=F32)
        for part in range(per_step):
            g = i * per_step + part
            taps = [out_ref[WK + tap, pl.ds(g, 1), :] for tap in range(4)]
            coefs = placed(strikes, taps, out_ref[COL, pl.ds(g, 1), :], (NK, LANES))
            for s in range(scenarios):
                piece = mixed[s * NK : (s + 1) * NK, part * LANES : (part + 1) * LANES]
                shift_ref[s, pl.ds(g, 1), :] = jnp.sum(piece * coefs, axis=0, keepdims=True)
        return carry

    lax.fori_loop(0, groups // per_step, some, 0)


def surface_kernel(slot, owned, per_step, message_ref, pre_ref, *refs):
    before_ref = refs[0] if len(refs) == 4 else None
    out_ref, table_ref, index_ref = refs[-3:]
    groups = pre_ref.shape[1]
    table_ref[0:WIDE, :] = message_ref[0:WIDE, :]
    table_ref[WIDE : WIDE + 3 * NK, :] = pltpu.roll(
        message_ref[0 : 3 * NK, :].astype(F32), (BLOCKS - 1) * owned, 1
    ).astype(BF16)
    extra = message_ref[WIDE : WIDE + EXTRA, 0 : 2 * LANES].astype(F32)
    betas = extra[0:1, 0:LANES] + extra[1:2, 0:LANES] + extra[2:3, 0:LANES]
    sub = 8
    for i in range(groups // sub):
        rows = pl.ds(i * sub, sub)
        held = pre_ref[SLOT, rows, :] == float(slot)
        local = pre_ref[PICK, rows, :]
        for h in range(HOT):
            hot = jnp.broadcast_to(extra[h : h + 1, LANES : 2 * LANES], (sub, LANES))
            local = jnp.where(local == float(owned + h), hot, local)
        looked = jnp.take_along_axis(
            jnp.broadcast_to(betas, (sub, LANES)),
            local.astype(jnp.int32),
            axis=1,
            mode="promise_in_bounds",
        )
        index_ref[rows, :] = jnp.where(held, local, -1.0)
        later = pl.ds(groups + i * sub, sub)
        other = 0.0 if before_ref is None else before_ref[later, :]
        out_ref[later, :] = jnp.where(held, looked, other)

    underlyings = lax.broadcasted_iota(jnp.int32, (owned, LANES), 0).astype(F32)
    strikes = lax.broadcasted_iota(jnp.int32, (NK, LANES), 0).astype(F32)
    expiries = lax.broadcasted_iota(jnp.int32, (2 * BAND, LANES), 0).astype(F32)
    zero = jnp.zeros((owned, LANES), BF16)

    def some(i, carry):
        sides = []
        for part in range(per_step):
            g = i * per_step + part
            index = jnp.broadcast_to(index_ref[pl.ds(g, 1), :], (owned, LANES))
            chosen = jnp.where(underlyings == index, 1.0, 0.0).astype(BF16)
            block = jnp.broadcast_to(pre_ref[BLK, pl.ds(g, 1), :], (owned, LANES)).astype(BF16)
            sides.append(
                jnp.concatenate(
                    [
                        jnp.where(block == jnp.asarray(j, BF16), chosen, zero)
                        for j in range(BLOCKS)
                    ],
                    axis=0,
                )
            )
        product = jnp.dot(
            table_ref[...], jnp.concatenate(sides, axis=1), preferred_element_type=F32
        )
        for part in range(per_step):
            g = i * per_step + part
            columns = slice(part * LANES, (part + 1) * LANES)
            taps = [pre_ref[WE + tap, pl.ds(g, 1), :] for tap in range(4)]
            mix = placed(expiries, taps, pre_ref[ROW, pl.ds(g, 1), :], (2 * BAND, LANES))
            curve = jnp.zeros((NK, LANES), F32)
            for a in range(REACH):
                curve = curve + product[a * NK : (a + 1) * NK, columns] * mix[a : a + 1, :]
            taps_k = [pre_ref[WK + tap, pl.ds(g, 1), :] for tap in range(4)]
            coefs = placed(strikes, taps_k, pre_ref[COL, pl.ds(g, 1), :], (NK, LANES))
            level = jnp.sum(curve * coefs, axis=0, keepdims=True)
            weight = (taps[0] + taps[1] + taps[2] + taps[3]) * (
                taps_k[0] + taps_k[1] + taps_k[2] + taps_k[3]
            )
            held = index_ref[pl.ds(g, 1), :] >= 0.0
            other = 0.0 if before_ref is None else before_ref[pl.ds(g, 1), :]
            out_ref[pl.ds(g, 1), :] = jnp.where(held, level - CENTRE * weight, other)
        return carry

    lax.fori_loop(0, groups // per_step, some, 0)


def value_kernel(part_ref, rest_ref, shift_ref, pre_ref, price_ref, vega_ref, delta_ref):
    scenarios, groups = shift_ref.shape[0], shift_ref.shape[1]
    sub = 8
    for i in range(groups // sub):
        rows = pl.ds(i * sub, sub)
        later = pl.ds(groups + i * sub, sub)
        level = part_ref[rows, :] + rest_ref[rows, :]
        slope = part_ref[later, :] + rest_ref[later, :]
        root_time = pre_ref[ROOT, rows, :]
        moneyness = pre_ref[MONEY, rows, :]
        growth = pre_ref[GROWTH, rows, :]
        scaled = pre_ref[CASH, rows, :]
        value = pre_ref[VALUE, rows, :]
        results = ([], [], [])
        for s in range(scenarios):
            spread = jnp.exp(level + slope * shift_ref[s, rows, :]) * root_time
            upper_d = -moneyness / spread + 0.5 * spread
            lower_d = upper_d - spread
            cdf_upper = 0.5 + 0.5 * lax.erf(upper_d * INV_ROOT_TWO)
            cdf_lower = 0.5 + 0.5 * lax.erf(lower_d * INV_ROOT_TWO)
            results[0].append(value * (cdf_upper - growth * cdf_lower))
            results[1].append(value * INV_ROOT_TAU * jnp.exp(-0.5 * upper_d * upper_d) * root_time)
            results[2].append(scaled * cdf_upper)
        for r in range(sub):
            columns = pl.ds((i * sub + r) * LANES, LANES)
            for ref, result in zip((price_ref, vega_ref, delta_ref), results):
                ref[:, columns] = jnp.concatenate([x[r : r + 1, :] for x in result], axis=0)


def shards(
    log_vol,
    beta,
    shock_table,
    scen_ids,
    hot_index,
    dest,
    pick,
    expiry_cell,
    strike_cell,
    frac_e,
    frac_k,
    notional,
    forward,
):
    n_trade = lax.axis_size("trade")
    n_scen = lax.axis_size("scen")
    slots = n_trade // n_scen
    owned = log_vol.shape[0]
    trades = pick.shape[0]
    groups = trades // LANES
    scenarios = scen_ids.shape[0]

    message = pl.pallas_call(
        pack_kernel,
        out_shape=pltpu.VMEM((WIDE + EXTRA, BLOCKS * owned), BF16),
        in_specs=[HBM] * 3,
        out_specs=VMEM,
        scratch_shapes=[
            pltpu.VMEM(log_vol.shape, F32),
            pltpu.VMEM((1, owned), F32),
            pltpu.SMEM(hot_index.shape, jnp.int32),
            pltpu.SemaphoreType.DMA((BLOCKS * owned // LANES,)),
            pltpu.SemaphoreType.DMA((2,)),
        ],
        compiler_params=params(16384),
    )(*in_hbm(hot_index, log_vol, beta.reshape(1, owned)))

    received = [None] * slots
    for k in reversed(range(slots)):
        pairs = [
            ((d ^ (q + k * n_scen)) * n_scen + q, d * n_scen + q)
            for d in range(n_trade)
            for q in range(n_scen)
        ]
        received[k] = lax.ppermute(message, ("trade", "scen"), pairs)

    dense = [
        column.reshape(groups, LANES)
        for column in (
            dest,
            pick,
            expiry_cell,
            strike_cell,
            frac_e,
            frac_k,
            notional,
            forward,
        )
    ]
    prepared, shift_level = pl.pallas_call(
        functools.partial(prepare_kernel, n_trade, n_scen, owned, PREPARE_STEP),
        out_shape=(
            pltpu.VMEM((PREPARED, groups, LANES), F32),
            pltpu.VMEM((scenarios, groups, LANES), F32),
        ),
        in_specs=[HBM] * 10,
        out_specs=(VMEM, VMEM),
        scratch_shapes=[
            pltpu.SMEM(scen_ids.shape, jnp.int32),
            pltpu.VMEM((4, groups, LANES), jnp.int32),
            pltpu.VMEM((4, groups, LANES), F32),
            pltpu.VMEM((scenarios, 16, NE * NK), BF16),
            pltpu.VMEM((scenarios * NK, NE), F32),
            pltpu.SemaphoreType.DMA((9,)),
            pltpu.SemaphoreType.DMA((scenarios,)),
        ],
        cost_estimate=pl.CostEstimate(flops=40_000_000, bytes_accessed=6_000_000, transcendentals=0),
        compiler_params=params(16384),
    )(*in_hbm(scen_ids, shock_table, *dense))

    partial_levels = None
    for k in range(slots):
        before = [] if partial_levels is None else [partial_levels]
        partial_levels = pl.pallas_call(
            functools.partial(surface_kernel, k, owned, SURFACE_STEP),
            out_shape=jax.ShapeDtypeStruct((2 * groups, LANES), F32),
            in_specs=[VMEM] * (2 + len(before)),
            out_specs=VMEM,
            scratch_shapes=[
                pltpu.VMEM((WIDE + 3 * NK, BLOCKS * owned), BF16),
                pltpu.VMEM((groups, LANES), F32),
            ],
            compiler_params=params(24576),
        )(received[k], prepared, *before)

    rest = jnp.zeros_like(partial_levels) if n_scen == 1 else None
    hop = n_scen // 2
    while hop:
        if rest is not None:
            partial_levels = partial_levels + rest
        rest = lax.ppermute(partial_levels, "scen", [(i, i ^ hop) for i in range(n_scen)])
        hop //= 2
    return pl.pallas_call(
        value_kernel,
        out_shape=(jax.ShapeDtypeStruct((scenarios, trades), F32),) * 3,
        in_specs=[VMEM] * 4,
        out_specs=(VMEM,) * 3,
        compiler_params=params(8192),
    )(partial_levels, rest, shift_level, prepared)


def solution(mesh):
    in_specs = (
        P("trade", None),
        P("trade"),
        P(),
        P("scen"),
        P("trade"),
        P("trade", None),
        P("trade"),
        P("trade"),
        P("trade"),
        P("trade"),
        P("trade"),
        P("trade"),
        P("trade"),
    )
    out_specs = (P("scen", "trade"), P("scen", "trade"), P("scen", "trade"))
    return jax.shard_map(shards, mesh=mesh, in_specs=in_specs, out_specs=out_specs, check_vma=False)
```

```python
import functools

import jax
import jax.numpy as jnp
from jax import lax
from jax.experimental import pallas as pl
from jax.experimental.pallas import tpu as pltpu
from jax.sharding import PartitionSpec as P

NE = 64
NK = 32
HOT = 2
LANES = 128
BAND = 8
BLOCKS = NE // BAND
TILES = BAND * NK // LANES
WIDE = BAND * NK
REACH = BAND + 3
EXTRA = 16
CENTRE = 1.4
PREPARE_STEP = 8
SHIFT_STEP = 32
SURFACE_STEP = 64

RATE = 0.03
INV_ROOT_TWO = 0.7071067811865476
INV_ROOT_TAU = 0.3989422804014327

VMEM = pl.BlockSpec(memory_space=pltpu.VMEM)
HBM = pl.BlockSpec(memory_space=pltpu.HBM)
F32 = jnp.float32
BF16 = jnp.bfloat16

(WE, FIRST, BLK, SLOT, PICK, BIAS) = (0, 4, 5, 6, 7, 8)
(ROOT, MONEY, GROWTH, CASH, VALUE) = (9, 10, 11, 12, 13)
PREPARED = 14


def spline_weights(offset):
    square = offset * offset
    offset_cube = square * offset
    return (
        0.5 * (2.0 * square - offset_cube - offset),
        0.5 * (3.0 * offset_cube - 5.0 * square + 2.0),
        0.5 * (4.0 * square - 3.0 * offset_cube + offset),
        0.5 * (offset_cube - square),
    )


def in_hbm(*arrays):
    return [pltpu.with_memory_space_constraint(x, pltpu.HBM) if x.size > 1 else x for x in arrays]


def params(kilobytes):
    return pltpu.CompilerParams(vmem_limit_bytes=kilobytes << 10)


def pack_kernel(hot_in, log_vol_in, beta_in, out_ref, log_vol_ref, beta_ref, hot_ref, sems, small):
    owned = log_vol_ref.shape[0]
    per_tile = LANES // owned
    steps = BLOCKS // per_tile
    width = log_vol_ref.shape[1] // steps
    copies = []
    for tile in range(steps):
        columns = pl.ds(tile * width, width)
        copies.append(
            pltpu.make_async_copy(
                log_vol_in.at[:, columns], log_vol_ref.at[:, columns], sems.at[tile]
            )
        )
    copies.append(pltpu.make_async_copy(beta_in, beta_ref, small.at[0]))
    copies.append(pltpu.make_async_copy(hot_in, hot_ref, small.at[1]))
    for copy in copies:
        copy.start()
    for tile in range(steps):
        copies[tile].wait()
        for half in range(TILES):
            first = [((tile * per_tile + i) * TILES + half) * LANES for i in range(per_tile)]
            stacked = jnp.concatenate([log_vol_ref[:, c : c + LANES] for c in first], axis=0)
            out_ref[half * LANES : (half + 1) * LANES, tile * LANES : (tile + 1) * LANES] = (
                jnp.transpose(stacked) + CENTRE
            ).astype(BF16)
    copies[steps].wait()
    copies[steps + 1].wait()
    row = lax.broadcasted_iota(jnp.int32, (EXTRA, LANES), 0)
    beta = jnp.broadcast_to(beta_ref[...], (EXTRA, owned))
    high = beta.astype(BF16).astype(F32)
    middle = (beta - high).astype(BF16).astype(F32)
    low = beta - high - middle
    zero = jnp.zeros((EXTRA, LANES), F32)
    row_b = row[:, 0:owned]
    pieces = jnp.where(row_b == 0, high, jnp.where(row_b == 1, middle, jnp.where(row_b == 2, low, 0.0)))
    hots = zero
    for i in range(HOT):
        hots = jnp.where(row == i, hot_ref[i].astype(F32), hots)
    out_ref[WIDE : WIDE + EXTRA, 0:LANES] = zero.astype(BF16)
    out_ref[WIDE : WIDE + EXTRA, 0:owned] = pieces.astype(BF16)
    out_ref[WIDE : WIDE + EXTRA, LANES : 2 * LANES] = hots.astype(BF16)
    for tile in range(2, BLOCKS // per_tile):
        out_ref[WIDE : WIDE + EXTRA, tile * LANES : (tile + 1) * LANES] = zero.astype(BF16)


def placed(position, weights, first, shape):
    distance = position - jnp.broadcast_to(first, shape)
    result = jnp.zeros(shape, F32)
    for tap in range(4):
        result = jnp.where(distance == float(tap), jnp.broadcast_to(weights[tap], shape), result)
    return result


def prepare_kernel(
    device_count,
    n_scen,
    owned,
    per_step,
    scen_in,
    shock_ref,
    *refs,
):
    whole, reals = refs[:4], refs[4:8]
    out_ref, mix_ref, coef_ref, matrix_ref = refs[8:12]
    scen_ref, whole_ref, real_ref, rows_ref, wide_ref, row_ref, tap_ref, sems, sem = refs[12:]
    groups = out_ref.shape[1]
    scenarios = rows_ref.shape[0]
    ids = pltpu.make_async_copy(scen_in, scen_ref, sems.at[8])
    ids.start()
    columns = []
    for i in range(4):
        columns.append(pltpu.make_async_copy(whole[i], whole_ref.at[i], sems.at[i]))
        columns.append(pltpu.make_async_copy(reals[i], real_ref.at[i], sems.at[4 + i]))
    for copy in columns:
        copy.start()
    ids.wait()
    copies = []
    for s in range(scenarios):
        first = pl.multiple_of(lax.shift_right_logical(scen_ref[s], 4) * 16, 16)
        copies.append(
            pltpu.make_async_copy(shock_ref.at[pl.ds(first, 16), :], rows_ref.at[s], sem.at[s])
        )
        copies[-1].start()
    for copy in columns:
        copy.wait()
    dest, pick, expiry, strike = [whole_ref[i] for i in range(4)]
    frac_e, frac_k, notional, forward = [real_ref[i] for i in range(4)]
    weights = [w.astype(BF16).astype(F32) for w in spline_weights(frac_e)]
    for tap in range(4):
        out_ref[WE + tap] = weights[tap]
    taps = spline_weights(frac_k)
    for tap in range(4):
        tap_ref[tap] = taps[tap]
    out_ref[BIAS] = CENTRE * (
        (weights[0] + weights[1] + weights[2] + weights[3]) * (taps[0] + taps[1] + taps[2] + taps[3])
    )
    first_row = expiry - 1
    block = lax.shift_right_logical(first_row, BAND.bit_length() - 1)
    row_ref[0] = (first_row - block * BAND).astype(F32)
    row_ref[1] = (strike - 1).astype(F32)
    out_ref[FIRST] = first_row.astype(F32)
    out_ref[BLK] = block.astype(F32)
    hot = pick - owned
    step = jnp.where(hot < 0, 0, jnp.where(hot < HOT, device_count - 1, 1))
    owner = (dest + step) & (device_count - 1)
    offset = owner ^ lax.axis_index("trade")
    mine = (offset & (n_scen - 1)) == lax.axis_index("scen")
    slot = lax.shift_right_logical(offset, n_scen.bit_length() - 1)
    out_ref[SLOT] = jnp.where(mine, slot, -1).astype(F32)
    out_ref[PICK] = jnp.where(hot < HOT, pick, pick - HOT).astype(F32)

    maturity = (expiry.astype(F32) + frac_e + 1.0) * (4.0 / NE)
    moneyness = (strike.astype(F32) + frac_k - 0.5 * (NK - 1)) / NK
    scaled = notional * jnp.exp(-RATE * maturity)
    out_ref[ROOT] = jnp.sqrt(maturity)
    out_ref[MONEY] = moneyness
    out_ref[GROWTH] = jnp.exp(moneyness)
    out_ref[CASH] = scaled
    out_ref[VALUE] = scaled * forward

    strikes = lax.broadcasted_iota(jnp.int32, (NK, LANES), 0).astype(F32)
    expiries = lax.broadcasted_iota(jnp.int32, (2 * BAND, LANES), 0).astype(F32)

    def some(i, carry):
        for part in range(per_step):
            g = i * per_step + part
            columns = pl.ds(pl.multiple_of(g * LANES, LANES), LANES)
            taps = [out_ref[WE + tap, pl.ds(g, 1), :] for tap in range(4)]
            mix_ref[:, columns] = placed(
                expiries, taps, row_ref[0, pl.ds(g, 1), :], (2 * BAND, LANES)
            )
            taps = [tap_ref[tap, pl.ds(g, 1), :] for tap in range(4)]
            coef_ref[:, columns] = placed(strikes, taps, row_ref[1, pl.ds(g, 1), :], (NK, LANES))
        return carry

    lax.fori_loop(0, groups // per_step, some, 0)

    tiles = NE * NK // LANES
    in_tile = LANES // NK
    line = lax.broadcasted_iota(jnp.int32, (16, NE * NK), 0)
    for s in range(scenarios):
        copies[s].wait()
        wanted = jnp.where(line == (scen_ref[s] & 15), rows_ref[s].astype(F32), 0.0)
        wanted = jnp.sum(wanted, axis=0, keepdims=True)
        stacked = jnp.concatenate(
            [wanted[:, i * LANES : (i + 1) * LANES] for i in range(tiles)], axis=0
        )
        turned = jnp.transpose(stacked)
        for i in range(in_tile):
            wide_ref[s * NK : (s + 1) * NK, i * tiles : (i + 1) * tiles] = turned[
                i * NK : (i + 1) * NK, :
            ]
    matrix_ref[...] = wide_ref[...].astype(BF16)


def shift_kernel(per_step, matrix_ref, pre_ref, coef_ref, after_ref, shift_ref):
    scenarios, groups = shift_ref.shape[0], shift_ref.shape[1]
    tiles = NE * NK // LANES
    in_tile = LANES // NK
    shift = matrix_ref[...]
    place = lax.broadcasted_iota(jnp.int32, (NE, LANES), 0)
    expiries = (
        (place & (tiles - 1)) * in_tile + lax.shift_right_logical(place, tiles.bit_length() - 1)
    ).astype(F32)

    def some(i, carry):
        sides = []
        for part in range(per_step):
            g = i * per_step + part
            taps = [pre_ref[WE + tap, pl.ds(g, 1), :] for tap in range(4)]
            sides.append(
                placed(expiries, taps, pre_ref[FIRST, pl.ds(g, 1), :], (NE, LANES)).astype(BF16)
            )
        mixed = jnp.dot(shift, jnp.concatenate(sides, axis=1), preferred_element_type=F32)
        for part in range(per_step):
            g = i * per_step + part
            coefs = coef_ref[:, pl.ds(pl.multiple_of(g * LANES, LANES), LANES)]
            for s in range(scenarios):
                piece = mixed[s * NK : (s + 1) * NK, part * LANES : (part + 1) * LANES]
                shift_ref[s, pl.ds(g, 1), :] = jnp.sum(piece * coefs, axis=0, keepdims=True)
        return carry

    lax.fori_loop(0, groups // per_step, some, 0)


def surface_kernel(slot, owned, per_step, message_ref, pre_ref, mix_ref, coef_ref, *refs):
    before_ref = refs[0] if len(refs) == 4 else None
    out_ref, table_ref, index_ref = refs[-3:]
    groups = pre_ref.shape[1]
    table_ref[0:WIDE, :] = message_ref[0:WIDE, :]
    table_ref[WIDE : WIDE + 3 * NK, :] = pltpu.roll(
        message_ref[0 : 3 * NK, :].astype(F32), (BLOCKS - 1) * owned, 1
    ).astype(BF16)
    extra = message_ref[WIDE : WIDE + EXTRA, 0 : 2 * LANES].astype(F32)
    betas = extra[0:1, 0:LANES] + extra[1:2, 0:LANES] + extra[2:3, 0:LANES]
    sub = 8
    for i in range(groups // sub):
        rows = pl.ds(i * sub, sub)
        held = pre_ref[SLOT, rows, :] == float(slot)
        local = pre_ref[PICK, rows, :]
        for h in range(HOT):
            hot = jnp.broadcast_to(extra[h : h + 1, LANES : 2 * LANES], (sub, LANES))
            local = jnp.where(local == float(owned + h), hot, local)
        looked = jnp.take_along_axis(
            jnp.broadcast_to(betas, (sub, LANES)),
            local.astype(jnp.int32),
            axis=1,
            mode="promise_in_bounds",
        )
        index_ref[rows, :] = jnp.where(held, local, -1.0)
        later = pl.ds(groups + i * sub, sub)
        other = 0.0 if before_ref is None else before_ref[later, :]
        out_ref[later, :] = jnp.where(held, looked, other)

    underlyings = lax.broadcasted_iota(jnp.int32, (owned, LANES), 0).astype(F32)
    zero = jnp.zeros((owned, LANES), BF16)

    def some(i, carry):
        sides = []
        for part in range(per_step):
            g = i * per_step + part
            index = jnp.broadcast_to(index_ref[pl.ds(g, 1), :], (owned, LANES))
            chosen = jnp.where(underlyings == index, 1.0, 0.0).astype(BF16)
            block = jnp.broadcast_to(pre_ref[BLK, pl.ds(g, 1), :], (owned, LANES)).astype(BF16)
            sides.append(
                jnp.concatenate(
                    [
                        jnp.where(block == jnp.asarray(j, BF16), chosen, zero)
                        for j in range(BLOCKS)
                    ],
                    axis=0,
                )
            )
        product = jnp.dot(
            table_ref[...], jnp.concatenate(sides, axis=1), preferred_element_type=F32
        )
        for part in range(per_step):
            g = i * per_step + part
            columns = slice(part * LANES, (part + 1) * LANES)
            here = pl.ds(pl.multiple_of(g * LANES, LANES), LANES)
            mix = mix_ref[:, here]
            curve = jnp.zeros((NK, LANES), F32)
            for a in range(REACH):
                curve = curve + product[a * NK : (a + 1) * NK, columns] * mix[a : a + 1, :]
            level = jnp.sum(curve * coef_ref[:, here], axis=0, keepdims=True)
            level = level - pre_ref[BIAS, pl.ds(g, 1), :]
            held = index_ref[pl.ds(g, 1), :] >= 0.0
            other = 0.0 if before_ref is None else before_ref[pl.ds(g, 1), :]
            out_ref[pl.ds(g, 1), :] = jnp.where(held, level, other)
        return carry

    lax.fori_loop(0, groups // per_step, some, 0)


def value_kernel(part_ref, rest_ref, shift_ref, pre_ref, price_ref, vega_ref, delta_ref):
    scenarios, groups = shift_ref.shape[0], shift_ref.shape[1]
    sub = 8
    for i in range(groups // sub):
        rows = pl.ds(i * sub, sub)
        later = pl.ds(groups + i * sub, sub)
        level = part_ref[rows, :] + rest_ref[rows, :]
        slope = part_ref[later, :] + rest_ref[later, :]
        root_time = pre_ref[ROOT, rows, :]
        moneyness = pre_ref[MONEY, rows, :]
        growth = pre_ref[GROWTH, rows, :]
        scaled = pre_ref[CASH, rows, :]
        value = pre_ref[VALUE, rows, :]
        results = ([], [], [])
        for s in range(scenarios):
            spread = jnp.exp(level + slope * shift_ref[s, rows, :]) * root_time
            upper_d = -moneyness / spread + 0.5 * spread
            lower_d = upper_d - spread
            cdf_upper = 0.5 + 0.5 * lax.erf(upper_d * INV_ROOT_TWO)
            cdf_lower = 0.5 + 0.5 * lax.erf(lower_d * INV_ROOT_TWO)
            results[0].append(value * (cdf_upper - growth * cdf_lower))
            results[1].append(value * INV_ROOT_TAU * jnp.exp(-0.5 * upper_d * upper_d) * root_time)
            results[2].append(scaled * cdf_upper)
        for r in range(sub):
            columns = pl.ds((i * sub + r) * LANES, LANES)
            for ref, result in zip((price_ref, vega_ref, delta_ref), results):
                ref[:, columns] = jnp.concatenate([x[r : r + 1, :] for x in result], axis=0)


def shards(
    log_vol,
    beta,
    shock_table,
    scen_ids,
    hot_index,
    dest,
    pick,
    expiry_cell,
    strike_cell,
    frac_e,
    frac_k,
    notional,
    forward,
):
    n_trade = lax.axis_size("trade")
    n_scen = lax.axis_size("scen")
    slots = n_trade // n_scen
    owned = log_vol.shape[0]
    trades = pick.shape[0]
    groups = trades // LANES
    scenarios = scen_ids.shape[0]

    message = pl.pallas_call(
        pack_kernel,
        out_shape=pltpu.VMEM((WIDE + EXTRA, BLOCKS * owned), BF16),
        in_specs=[HBM] * 3,
        out_specs=VMEM,
        scratch_shapes=[
            pltpu.VMEM(log_vol.shape, F32),
            pltpu.VMEM((1, owned), F32),
            pltpu.SMEM(hot_index.shape, jnp.int32),
            pltpu.SemaphoreType.DMA((BLOCKS * owned // LANES,)),
            pltpu.SemaphoreType.DMA((2,)),
        ],
        compiler_params=params(16384),
    )(*in_hbm(hot_index, log_vol, beta.reshape(1, owned)))

    received = [None] * slots
    for k in reversed(range(slots)):
        pairs = [
            ((d ^ (q + k * n_scen)) * n_scen + q, d * n_scen + q)
            for d in range(n_trade)
            for q in range(n_scen)
        ]
        received[k] = lax.ppermute(message, ("trade", "scen"), pairs)

    dense = [
        column.reshape(groups, LANES)
        for column in (
            dest,
            pick,
            expiry_cell,
            strike_cell,
            frac_e,
            frac_k,
            notional,
            forward,
        )
    ]
    prepared, mix, coefs, matrix = pl.pallas_call(
        functools.partial(prepare_kernel, n_trade, n_scen, owned, PREPARE_STEP),
        out_shape=(
            pltpu.VMEM((PREPARED, groups, LANES), F32),
            pltpu.VMEM((2 * BAND, trades), F32),
            pltpu.VMEM((NK, trades), F32),
            pltpu.VMEM((scenarios * NK, NE), BF16),
        ),
        in_specs=[HBM] * 10,
        out_specs=(VMEM,) * 4,
        scratch_shapes=[
            pltpu.SMEM(scen_ids.shape, jnp.int32),
            pltpu.VMEM((4, groups, LANES), jnp.int32),
            pltpu.VMEM((4, groups, LANES), F32),
            pltpu.VMEM((scenarios, 16, NE * NK), BF16),
            pltpu.VMEM((scenarios * NK, NE), F32),
            pltpu.VMEM((2, groups, LANES), F32),
            pltpu.VMEM((4, groups, LANES), F32),
            pltpu.SemaphoreType.DMA((9,)),
            pltpu.SemaphoreType.DMA((scenarios,)),
        ],
        cost_estimate=pl.CostEstimate(flops=40_000_000, bytes_accessed=6_000_000, transcendentals=0),
        compiler_params=params(16384),
    )(*in_hbm(scen_ids, shock_table, *dense))

    partial_levels = None
    for k in reversed(range(slots)):
        before = [] if partial_levels is None else [partial_levels]
        partial_levels = pl.pallas_call(
            functools.partial(surface_kernel, k, owned, SURFACE_STEP),
            out_shape=jax.ShapeDtypeStruct((2 * groups, LANES), F32),
            in_specs=[VMEM] * (4 + len(before)),
            out_specs=VMEM,
            scratch_shapes=[
                pltpu.VMEM((WIDE + 3 * NK, BLOCKS * owned), BF16),
                pltpu.VMEM((groups, LANES), F32),
            ],
            compiler_params=params(32768),
        )(received[k], prepared, mix, coefs, *before)

    shift_level = pl.pallas_call(
        functools.partial(shift_kernel, SHIFT_STEP),
        out_shape=pltpu.VMEM((scenarios, groups, LANES), F32),
        in_specs=[VMEM] * 3 + [pl.BlockSpec(memory_space=pl.ANY)],
        out_specs=VMEM,
        cost_estimate=pl.CostEstimate(flops=40_000_000, bytes_accessed=2_000_000, transcendentals=0),
        compiler_params=params(16384),
    )(matrix, prepared, coefs, partial_levels)

    rest = jnp.zeros_like(partial_levels) if n_scen == 1 else None
    hop = n_scen // 2
    while hop:
        if rest is not None:
            partial_levels, shift_level = lax.optimization_barrier(
                (partial_levels + rest, shift_level)
            )
        rest = lax.ppermute(partial_levels, "scen", [(i, i ^ hop) for i in range(n_scen)])
        hop //= 2
    return pl.pallas_call(
        value_kernel,
        out_shape=(jax.ShapeDtypeStruct((scenarios, trades), F32),) * 3,
        in_specs=[VMEM] * 4,
        out_specs=(VMEM,) * 3,
        compiler_params=params(8192),
    )(partial_levels, rest, shift_level, prepared)


def solution(mesh):
    in_specs = (
        P("trade", None),
        P("trade"),
        P(),
        P("scen"),
        P("trade"),
        P("trade", None),
        P("trade"),
        P("trade"),
        P("trade"),
        P("trade"),
        P("trade"),
        P("trade"),
        P("trade"),
    )
    out_specs = (P("scen", "trade"), P("scen", "trade"), P("scen", "trade"))
    return jax.shard_map(shards, mesh=mesh, in_specs=in_specs, out_specs=out_specs, check_vma=False)
```

```python
import functools

import jax
import jax.numpy as jnp
from jax import lax
from jax.experimental import pallas as pl
from jax.experimental.pallas import tpu as pltpu
from jax.sharding import PartitionSpec as P

NE = 64
NK = 32
HOT = 2
LANES = 128
BAND = 8
BLOCKS = NE // BAND
TILES = BAND * NK // LANES
WIDE = BAND * NK
REACH = BAND + 3
EXTRA = 16
CENTRE = 1.4
PREPARE_STEP = 8
SHIFT_STEP = 32
SURFACE_STEP = 64

RATE = 0.03
INV_ROOT_TWO = 0.7071067811865476
INV_ROOT_TAU = 0.3989422804014327

VMEM = pl.BlockSpec(memory_space=pltpu.VMEM)
HBM = pl.BlockSpec(memory_space=pltpu.HBM)
F32 = jnp.float32
BF16 = jnp.bfloat16

(WE, FIRST, BLK, SLOT, PICK, BIAS) = (0, 4, 5, 6, 7, 8)
(ROOT, MONEY, GROWTH, CASH, VALUE) = (9, 10, 11, 12, 13)
PREPARED = 14


def spline_weights(offset):
    square = offset * offset
    offset_cube = square * offset
    return (
        0.5 * (2.0 * square - offset_cube - offset),
        0.5 * (3.0 * offset_cube - 5.0 * square + 2.0),
        0.5 * (4.0 * square - 3.0 * offset_cube + offset),
        0.5 * (offset_cube - square),
    )


def in_hbm(*arrays):
    return [pltpu.with_memory_space_constraint(x, pltpu.HBM) if x.size > 1 else x for x in arrays]


def params(kilobytes):
    return pltpu.CompilerParams(vmem_limit_bytes=kilobytes << 10)


def pack_kernel(hot_in, log_vol_in, beta_in, out_ref, log_vol_ref, beta_ref, hot_ref, sems, small):
    owned = log_vol_ref.shape[0]
    per_tile = LANES // owned
    steps = BLOCKS // per_tile
    width = log_vol_ref.shape[1] // steps
    copies = []
    for tile in range(steps):
        columns = pl.ds(tile * width, width)
        copies.append(
            pltpu.make_async_copy(
                log_vol_in.at[:, columns], log_vol_ref.at[:, columns], sems.at[tile]
            )
        )
    copies.append(pltpu.make_async_copy(beta_in, beta_ref, small.at[0]))
    copies.append(pltpu.make_async_copy(hot_in, hot_ref, small.at[1]))
    for copy in copies:
        copy.start()
    for tile in range(steps):
        copies[tile].wait()
        for half in range(TILES):
            first = [((tile * per_tile + i) * TILES + half) * LANES for i in range(per_tile)]
            stacked = jnp.concatenate([log_vol_ref[:, c : c + LANES] for c in first], axis=0)
            out_ref[half * LANES : (half + 1) * LANES, tile * LANES : (tile + 1) * LANES] = (
                jnp.transpose(stacked) + CENTRE
            ).astype(BF16)
    copies[steps].wait()
    copies[steps + 1].wait()
    row = lax.broadcasted_iota(jnp.int32, (EXTRA, LANES), 0)
    beta = jnp.broadcast_to(beta_ref[...], (EXTRA, owned))
    high = beta.astype(BF16).astype(F32)
    middle = (beta - high).astype(BF16).astype(F32)
    low = beta - high - middle
    zero = jnp.zeros((EXTRA, LANES), F32)
    row_b = row[:, 0:owned]
    pieces = jnp.where(row_b == 0, high, jnp.where(row_b == 1, middle, jnp.where(row_b == 2, low, 0.0)))
    hots = zero
    for i in range(HOT):
        hots = jnp.where(row == i, hot_ref[i].astype(F32), hots)
    out_ref[WIDE : WIDE + EXTRA, 0:LANES] = zero.astype(BF16)
    out_ref[WIDE : WIDE + EXTRA, 0:owned] = pieces.astype(BF16)
    out_ref[WIDE : WIDE + EXTRA, LANES : 2 * LANES] = hots.astype(BF16)
    for tile in range(2, BLOCKS // per_tile):
        out_ref[WIDE : WIDE + EXTRA, tile * LANES : (tile + 1) * LANES] = zero.astype(BF16)


def placed(position, weights, first, shape):
    distance = position - jnp.broadcast_to(first, shape)
    result = jnp.zeros(shape, F32)
    for tap in range(4):
        result = jnp.where(distance == float(tap), jnp.broadcast_to(weights[tap], shape), result)
    return result


def prepare_kernel(
    device_count,
    n_scen,
    owned,
    per_step,
    scen_in,
    shock_ref,
    *refs,
):
    whole, reals = refs[:4], refs[4:8]
    out_ref, mix_ref, coef_ref, matrix_ref = refs[8:12]
    scen_ref, whole_ref, real_ref, rows_ref, wide_ref, row_ref, tap_ref, sems, sem = refs[12:]
    groups = out_ref.shape[1]
    scenarios = rows_ref.shape[0]
    ids = pltpu.make_async_copy(scen_in, scen_ref, sems.at[8])
    ids.start()
    columns = []
    for i in range(4):
        columns.append(pltpu.make_async_copy(whole[i], whole_ref.at[i], sems.at[i]))
        columns.append(pltpu.make_async_copy(reals[i], real_ref.at[i], sems.at[4 + i]))
    for copy in columns:
        copy.start()
    ids.wait()
    copies = []
    for s in range(scenarios):
        first = pl.multiple_of(lax.shift_right_logical(scen_ref[s], 4) * 16, 16)
        copies.append(
            pltpu.make_async_copy(shock_ref.at[pl.ds(first, 16), :], rows_ref.at[s], sem.at[s])
        )
        copies[-1].start()
    for copy in columns:
        copy.wait()
    dest, pick, expiry, strike = [whole_ref[i] for i in range(4)]
    frac_e, frac_k, notional, forward = [real_ref[i] for i in range(4)]
    weights = [w.astype(BF16).astype(F32) for w in spline_weights(frac_e)]
    for tap in range(4):
        out_ref[WE + tap] = weights[tap]
    taps = spline_weights(frac_k)
    for tap in range(4):
        tap_ref[tap] = taps[tap]
    out_ref[BIAS] = CENTRE * (
        (weights[0] + weights[1] + weights[2] + weights[3]) * (taps[0] + taps[1] + taps[2] + taps[3])
    )
    first_row = expiry - 1
    block = lax.shift_right_logical(first_row, BAND.bit_length() - 1)
    row_ref[0] = (first_row - block * BAND).astype(F32)
    row_ref[1] = (strike - 1).astype(F32)
    out_ref[FIRST] = first_row.astype(F32)
    out_ref[BLK] = block.astype(F32)
    hot = pick - owned
    step = jnp.where(hot < 0, 0, jnp.where(hot < HOT, device_count - 1, 1))
    owner = (dest + step) & (device_count - 1)
    offset = owner ^ lax.axis_index("trade")
    scen_place = lax.axis_index("scen")
    ring = lax.shift_right_logical(offset, n_scen.bit_length() - 1)
    mine = ((offset & (n_scen - 1)) ^ ((ring & 1) * (n_scen // 2))) == scen_place
    slot = ring ^ (scen_place & (device_count // n_scen - 1) & 1)
    out_ref[SLOT] = jnp.where(mine, slot, -1).astype(F32)
    out_ref[PICK] = jnp.where(hot < HOT, pick, pick - HOT).astype(F32)

    maturity = (expiry.astype(F32) + frac_e + 1.0) * (4.0 / NE)
    moneyness = (strike.astype(F32) + frac_k - 0.5 * (NK - 1)) / NK
    scaled = notional * jnp.exp(-RATE * maturity)
    out_ref[ROOT] = jnp.sqrt(maturity)
    out_ref[MONEY] = moneyness
    out_ref[GROWTH] = jnp.exp(moneyness)
    out_ref[CASH] = scaled
    out_ref[VALUE] = scaled * forward

    strikes = lax.broadcasted_iota(jnp.int32, (NK, LANES), 0).astype(F32)
    expiries = lax.broadcasted_iota(jnp.int32, (2 * BAND, LANES), 0).astype(F32)

    def some(i, carry):
        for part in range(per_step):
            g = i * per_step + part
            columns = pl.ds(pl.multiple_of(g * LANES, LANES), LANES)
            taps = [out_ref[WE + tap, pl.ds(g, 1), :] for tap in range(4)]
            mix_ref[:, columns] = placed(
                expiries, taps, row_ref[0, pl.ds(g, 1), :], (2 * BAND, LANES)
            )
            taps = [tap_ref[tap, pl.ds(g, 1), :] for tap in range(4)]
            coef_ref[:, columns] = placed(strikes, taps, row_ref[1, pl.ds(g, 1), :], (NK, LANES))
        return carry

    lax.fori_loop(0, groups // per_step, some, 0)

    tiles = NE * NK // LANES
    in_tile = LANES // NK
    line = lax.broadcasted_iota(jnp.int32, (16, NE * NK), 0)
    for s in range(scenarios):
        copies[s].wait()
        wanted = jnp.where(line == (scen_ref[s] & 15), rows_ref[s].astype(F32), 0.0)
        wanted = jnp.sum(wanted, axis=0, keepdims=True)
        stacked = jnp.concatenate(
            [wanted[:, i * LANES : (i + 1) * LANES] for i in range(tiles)], axis=0
        )
        turned = jnp.transpose(stacked)
        for i in range(in_tile):
            wide_ref[s * NK : (s + 1) * NK, i * tiles : (i + 1) * tiles] = turned[
                i * NK : (i + 1) * NK, :
            ]
    matrix_ref[...] = wide_ref[...].astype(BF16)


def shift_kernel(per_step, matrix_ref, pre_ref, coef_ref, after_ref, shift_ref):
    scenarios, groups = shift_ref.shape[0], shift_ref.shape[1]
    tiles = NE * NK // LANES
    in_tile = LANES // NK
    shift = matrix_ref[...]
    place = lax.broadcasted_iota(jnp.int32, (NE, LANES), 0)
    expiries = (
        (place & (tiles - 1)) * in_tile + lax.shift_right_logical(place, tiles.bit_length() - 1)
    ).astype(F32)

    def some(i, carry):
        sides = []
        for part in range(per_step):
            g = i * per_step + part
            taps = [pre_ref[WE + tap, pl.ds(g, 1), :] for tap in range(4)]
            sides.append(
                placed(expiries, taps, pre_ref[FIRST, pl.ds(g, 1), :], (NE, LANES)).astype(BF16)
            )
        mixed = jnp.dot(shift, jnp.concatenate(sides, axis=1), preferred_element_type=F32)
        for part in range(per_step):
            g = i * per_step + part
            coefs = coef_ref[:, pl.ds(pl.multiple_of(g * LANES, LANES), LANES)]
            for s in range(scenarios):
                piece = mixed[s * NK : (s + 1) * NK, part * LANES : (part + 1) * LANES]
                shift_ref[s, pl.ds(g, 1), :] = jnp.sum(piece * coefs, axis=0, keepdims=True)
        return carry

    lax.fori_loop(0, groups // per_step, some, 0)


def surface_kernel(slot, owned, per_step, message_ref, pre_ref, mix_ref, coef_ref, *refs):
    before_ref = refs[0] if len(refs) == 4 else None
    out_ref, table_ref, index_ref = refs[-3:]
    groups = pre_ref.shape[1]
    table_ref[0:WIDE, :] = message_ref[0:WIDE, :]
    table_ref[WIDE : WIDE + 3 * NK, :] = pltpu.roll(
        message_ref[0 : 3 * NK, :].astype(F32), (BLOCKS - 1) * owned, 1
    ).astype(BF16)
    extra = message_ref[WIDE : WIDE + EXTRA, 0 : 2 * LANES].astype(F32)
    betas = extra[0:1, 0:LANES] + extra[1:2, 0:LANES] + extra[2:3, 0:LANES]
    sub = 8
    for i in range(groups // sub):
        rows = pl.ds(i * sub, sub)
        held = pre_ref[SLOT, rows, :] == float(slot)
        local = pre_ref[PICK, rows, :]
        for h in range(HOT):
            hot = jnp.broadcast_to(extra[h : h + 1, LANES : 2 * LANES], (sub, LANES))
            local = jnp.where(local == float(owned + h), hot, local)
        looked = jnp.take_along_axis(
            jnp.broadcast_to(betas, (sub, LANES)),
            local.astype(jnp.int32),
            axis=1,
            mode="promise_in_bounds",
        )
        index_ref[rows, :] = jnp.where(held, local, -1.0)
        later = pl.ds(groups + i * sub, sub)
        other = 0.0 if before_ref is None else before_ref[later, :]
        out_ref[later, :] = jnp.where(held, looked, other)

    underlyings = lax.broadcasted_iota(jnp.int32, (owned, LANES), 0).astype(F32)
    zero = jnp.zeros((owned, LANES), BF16)

    def some(i, carry):
        sides = []
        for part in range(per_step):
            g = i * per_step + part
            index = jnp.broadcast_to(index_ref[pl.ds(g, 1), :], (owned, LANES))
            chosen = jnp.where(underlyings == index, 1.0, 0.0).astype(BF16)
            block = jnp.broadcast_to(pre_ref[BLK, pl.ds(g, 1), :], (owned, LANES)).astype(BF16)
            sides.append(
                jnp.concatenate(
                    [
                        jnp.where(block == jnp.asarray(j, BF16), chosen, zero)
                        for j in range(BLOCKS)
                    ],
                    axis=0,
                )
            )
        product = jnp.dot(
            table_ref[...], jnp.concatenate(sides, axis=1), preferred_element_type=F32
        )
        for part in range(per_step):
            g = i * per_step + part
            columns = slice(part * LANES, (part + 1) * LANES)
            here = pl.ds(pl.multiple_of(g * LANES, LANES), LANES)
            mix = mix_ref[:, here]
            curve = jnp.zeros((NK, LANES), F32)
            for a in range(REACH):
                curve = curve + product[a * NK : (a + 1) * NK, columns] * mix[a : a + 1, :]
            level = jnp.sum(curve * coef_ref[:, here], axis=0, keepdims=True)
            level = level - pre_ref[BIAS, pl.ds(g, 1), :]
            held = index_ref[pl.ds(g, 1), :] >= 0.0
            other = 0.0 if before_ref is None else before_ref[pl.ds(g, 1), :]
            out_ref[pl.ds(g, 1), :] = jnp.where(held, level, other)
        return carry

    lax.fori_loop(0, groups // per_step, some, 0)


def value_kernel(part_ref, rest_ref, shift_ref, pre_ref, price_ref, vega_ref, delta_ref):
    scenarios, groups = shift_ref.shape[0], shift_ref.shape[1]
    sub = 8
    for i in range(groups // sub):
        rows = pl.ds(i * sub, sub)
        later = pl.ds(groups + i * sub, sub)
        level = part_ref[rows, :] + rest_ref[rows, :]
        slope = part_ref[later, :] + rest_ref[later, :]
        root_time = pre_ref[ROOT, rows, :]
        moneyness = pre_ref[MONEY, rows, :]
        growth = pre_ref[GROWTH, rows, :]
        scaled = pre_ref[CASH, rows, :]
        value = pre_ref[VALUE, rows, :]
        results = ([], [], [])
        for s in range(scenarios):
            spread = jnp.exp(level + slope * shift_ref[s, rows, :]) * root_time
            upper_d = -moneyness / spread + 0.5 * spread
            lower_d = upper_d - spread
            cdf_upper = 0.5 + 0.5 * lax.erf(upper_d * INV_ROOT_TWO)
            cdf_lower = 0.5 + 0.5 * lax.erf(lower_d * INV_ROOT_TWO)
            results[0].append(value * (cdf_upper - growth * cdf_lower))
            results[1].append(value * INV_ROOT_TAU * jnp.exp(-0.5 * upper_d * upper_d) * root_time)
            results[2].append(scaled * cdf_upper)
        for r in range(sub):
            columns = pl.ds((i * sub + r) * LANES, LANES)
            for ref, result in zip((price_ref, vega_ref, delta_ref), results):
                ref[:, columns] = jnp.concatenate([x[r : r + 1, :] for x in result], axis=0)


def shards(
    log_vol,
    beta,
    shock_table,
    scen_ids,
    hot_index,
    dest,
    pick,
    expiry_cell,
    strike_cell,
    frac_e,
    frac_k,
    notional,
    forward,
):
    n_trade = lax.axis_size("trade")
    n_scen = lax.axis_size("scen")
    slots = n_trade // n_scen
    owned = log_vol.shape[0]
    trades = pick.shape[0]
    groups = trades // LANES
    scenarios = scen_ids.shape[0]

    message = pl.pallas_call(
        pack_kernel,
        out_shape=pltpu.VMEM((WIDE + EXTRA, BLOCKS * owned), BF16),
        in_specs=[HBM] * 3,
        out_specs=VMEM,
        scratch_shapes=[
            pltpu.VMEM(log_vol.shape, F32),
            pltpu.VMEM((1, owned), F32),
            pltpu.SMEM(hot_index.shape, jnp.int32),
            pltpu.SemaphoreType.DMA((BLOCKS * owned // LANES,)),
            pltpu.SemaphoreType.DMA((2,)),
        ],
        compiler_params=params(16384),
    )(*in_hbm(hot_index, log_vol, beta.reshape(1, owned)))

    received = [None] * slots
    for k in reversed(range(slots)):
        pairs = []
        for d in range(n_trade):
            for q in range(n_scen):
                ring = k ^ (q & (slots - 1) & 1)
                offset = ring * n_scen + (q ^ ((ring & 1) * (n_scen // 2)))
                pairs.append(((d ^ offset) * n_scen + q, d * n_scen + q))
        received[k] = lax.ppermute(message, ("trade", "scen"), pairs)

    dense = [
        column.reshape(groups, LANES)
        for column in (
            dest,
            pick,
            expiry_cell,
            strike_cell,
            frac_e,
            frac_k,
            notional,
            forward,
        )
    ]
    prepared, mix, coefs, matrix = pl.pallas_call(
        functools.partial(prepare_kernel, n_trade, n_scen, owned, PREPARE_STEP),
        out_shape=(
            pltpu.VMEM((PREPARED, groups, LANES), F32),
            pltpu.VMEM((2 * BAND, trades), F32),
            pltpu.VMEM((NK, trades), F32),
            pltpu.VMEM((scenarios * NK, NE), BF16),
        ),
        in_specs=[HBM] * 10,
        out_specs=(VMEM,) * 4,
        scratch_shapes=[
            pltpu.SMEM(scen_ids.shape, jnp.int32),
            pltpu.VMEM((4, groups, LANES), jnp.int32),
            pltpu.VMEM((4, groups, LANES), F32),
            pltpu.VMEM((scenarios, 16, NE * NK), BF16),
            pltpu.VMEM((scenarios * NK, NE), F32),
            pltpu.VMEM((2, groups, LANES), F32),
            pltpu.VMEM((4, groups, LANES), F32),
            pltpu.SemaphoreType.DMA((9,)),
            pltpu.SemaphoreType.DMA((scenarios,)),
        ],
        cost_estimate=pl.CostEstimate(flops=40_000_000, bytes_accessed=6_000_000, transcendentals=0),
        compiler_params=params(16384),
    )(*in_hbm(scen_ids, shock_table, *dense))

    partial_levels = None
    for k in reversed(range(slots)):
        before = [] if partial_levels is None else [partial_levels]
        partial_levels = pl.pallas_call(
            functools.partial(surface_kernel, k, owned, SURFACE_STEP),
            out_shape=jax.ShapeDtypeStruct((2 * groups, LANES), F32),
            in_specs=[VMEM] * (4 + len(before)),
            out_specs=VMEM,
            scratch_shapes=[
                pltpu.VMEM((WIDE + 3 * NK, BLOCKS * owned), BF16),
                pltpu.VMEM((groups, LANES), F32),
            ],
            compiler_params=params(32768),
        )(received[k], prepared, mix, coefs, *before)

    shift_level = pl.pallas_call(
        functools.partial(shift_kernel, SHIFT_STEP),
        out_shape=pltpu.VMEM((scenarios, groups, LANES), F32),
        in_specs=[VMEM] * 3 + [pl.BlockSpec(memory_space=pl.ANY)],
        out_specs=VMEM,
        cost_estimate=pl.CostEstimate(flops=40_000_000, bytes_accessed=2_000_000, transcendentals=0),
        compiler_params=params(16384),
    )(matrix, prepared, coefs, partial_levels)

    rest = jnp.zeros_like(partial_levels) if n_scen == 1 else None
    hop = n_scen // 2
    while hop:
        if rest is not None:
            partial_levels, shift_level = lax.optimization_barrier(
                (partial_levels + rest, shift_level)
            )
        rest = lax.ppermute(partial_levels, "scen", [(i, i ^ hop) for i in range(n_scen)])
        hop //= 2
    return pl.pallas_call(
        value_kernel,
        out_shape=(jax.ShapeDtypeStruct((scenarios, trades), F32),) * 3,
        in_specs=[VMEM] * 4,
        out_specs=(VMEM,) * 3,
        compiler_params=params(8192),
    )(partial_levels, rest, shift_level, prepared)


def solution(mesh):
    in_specs = (
        P("trade", None),
        P("trade"),
        P(),
        P("scen"),
        P("trade"),
        P("trade", None),
        P("trade"),
        P("trade"),
        P("trade"),
        P("trade"),
        P("trade"),
        P("trade"),
        P("trade"),
    )
    out_specs = (P("scen", "trade"), P("scen", "trade"), P("scen", "trade"))
    return jax.shard_map(shards, mesh=mesh, in_specs=in_specs, out_specs=out_specs, check_vma=False)
```

```python
import functools

import jax
import jax.numpy as jnp
from jax import lax
from jax.experimental import pallas as pl
from jax.experimental.pallas import tpu as pltpu
from jax.sharding import PartitionSpec as P

NE = 64
NK = 32
HOT = 2
LANES = 128
BAND = 8
BLOCKS = NE // BAND
TILES = BAND * NK // LANES
WIDE = BAND * NK
REACH = BAND + 3
EXTRA = 16
CENTRE = 1.4
PREPARE_STEP = 8
SHIFT_STEP = 32
SURFACE_STEP = 64

RATE = 0.03
INV_ROOT_TWO = 0.7071067811865476
INV_ROOT_TAU = 0.3989422804014327

VMEM = pl.BlockSpec(memory_space=pltpu.VMEM)
HBM = pl.BlockSpec(memory_space=pltpu.HBM)
F32 = jnp.float32
BF16 = jnp.bfloat16

(WE, FIRST, BLK, SLOT, PICK, BIAS) = (0, 4, 5, 6, 7, 8)
(ROOT, MONEY, GROWTH, CASH, VALUE) = (9, 10, 11, 12, 13)
PREPARED = 14


def spline_weights(offset):
    square = offset * offset
    offset_cube = square * offset
    return (
        0.5 * (2.0 * square - offset_cube - offset),
        0.5 * (3.0 * offset_cube - 5.0 * square + 2.0),
        0.5 * (4.0 * square - 3.0 * offset_cube + offset),
        0.5 * (offset_cube - square),
    )


def in_hbm(*arrays):
    return [pltpu.with_memory_space_constraint(x, pltpu.HBM) if x.size > 1 else x for x in arrays]


def params(kilobytes):
    return pltpu.CompilerParams(vmem_limit_bytes=kilobytes << 10)


def pack_kernel(hot_in, log_vol_in, beta_in, out_ref, log_vol_ref, beta_ref, hot_ref, sems, small):
    owned = log_vol_ref.shape[0]
    per_tile = LANES // owned
    steps = BLOCKS // per_tile
    width = log_vol_ref.shape[1] // steps
    copies = []
    for tile in range(steps):
        columns = pl.ds(tile * width, width)
        copies.append(
            pltpu.make_async_copy(
                log_vol_in.at[:, columns], log_vol_ref.at[:, columns], sems.at[tile]
            )
        )
    copies.append(pltpu.make_async_copy(beta_in, beta_ref, small.at[0]))
    copies.append(pltpu.make_async_copy(hot_in, hot_ref, small.at[1]))
    for copy in copies:
        copy.start()
    for tile in range(steps):
        copies[tile].wait()
        for half in range(TILES):
            first = [((tile * per_tile + i) * TILES + half) * LANES for i in range(per_tile)]
            stacked = jnp.concatenate([log_vol_ref[:, c : c + LANES] for c in first], axis=0)
            out_ref[half * LANES : (half + 1) * LANES, tile * LANES : (tile + 1) * LANES] = (
                jnp.transpose(stacked) + CENTRE
            ).astype(BF16)
    copies[steps].wait()
    copies[steps + 1].wait()
    row = lax.broadcasted_iota(jnp.int32, (EXTRA, LANES), 0)
    beta = jnp.broadcast_to(beta_ref[...], (EXTRA, owned))
    high = beta.astype(BF16).astype(F32)
    middle = (beta - high).astype(BF16).astype(F32)
    low = beta - high - middle
    zero = jnp.zeros((EXTRA, LANES), F32)
    row_b = row[:, 0:owned]
    pieces = jnp.where(row_b == 0, high, jnp.where(row_b == 1, middle, jnp.where(row_b == 2, low, 0.0)))
    hots = zero
    for i in range(HOT):
        hots = jnp.where(row == i, hot_ref[i].astype(F32), hots)
    out_ref[WIDE : WIDE + EXTRA, 0:LANES] = zero.astype(BF16)
    out_ref[WIDE : WIDE + EXTRA, 0:owned] = pieces.astype(BF16)
    out_ref[WIDE : WIDE + EXTRA, LANES : 2 * LANES] = hots.astype(BF16)
    for tile in range(2, BLOCKS // per_tile):
        out_ref[WIDE : WIDE + EXTRA, tile * LANES : (tile + 1) * LANES] = zero.astype(BF16)


def placed(position, weights, first, shape):
    distance = position - jnp.broadcast_to(first, shape)
    result = jnp.zeros(shape, F32)
    for tap in range(4):
        result = jnp.where(distance == float(tap), jnp.broadcast_to(weights[tap], shape), result)
    return result


def prepare_kernel(
    device_count,
    n_scen,
    owned,
    per_step,
    scen_in,
    shock_ref,
    *refs,
):
    whole, reals = refs[:4], refs[4:8]
    out_ref, mix_ref, coef_ref, matrix_ref = refs[8:12]
    scen_ref, whole_ref, real_ref, rows_ref, wide_ref, row_ref, tap_ref, sems, sem = refs[12:]
    groups = out_ref.shape[1]
    scenarios = rows_ref.shape[0]
    ids = pltpu.make_async_copy(scen_in, scen_ref, sems.at[8])
    ids.start()
    columns = []
    for i in range(4):
        columns.append(pltpu.make_async_copy(whole[i], whole_ref.at[i], sems.at[i]))
        columns.append(pltpu.make_async_copy(reals[i], real_ref.at[i], sems.at[4 + i]))
    for copy in columns:
        copy.start()
    ids.wait()
    copies = []
    for s in range(scenarios):
        first = pl.multiple_of(lax.shift_right_logical(scen_ref[s], 4) * 16, 16)
        copies.append(
            pltpu.make_async_copy(shock_ref.at[pl.ds(first, 16), :], rows_ref.at[s], sem.at[s])
        )
        copies[-1].start()
    for copy in columns:
        copy.wait()
    dest, pick, expiry, strike = [whole_ref[i] for i in range(4)]
    frac_e, frac_k, notional, forward = [real_ref[i] for i in range(4)]
    weights = [w.astype(BF16).astype(F32) for w in spline_weights(frac_e)]
    for tap in range(4):
        out_ref[WE + tap] = weights[tap]
    taps = spline_weights(frac_k)
    for tap in range(4):
        tap_ref[tap] = taps[tap]
    out_ref[BIAS] = CENTRE * (
        (weights[0] + weights[1] + weights[2] + weights[3]) * (taps[0] + taps[1] + taps[2] + taps[3])
    )
    first_row = expiry - 1
    block = lax.shift_right_logical(first_row, BAND.bit_length() - 1)
    row_ref[0] = (first_row - block * BAND).astype(F32)
    row_ref[1] = (strike - 1).astype(F32)
    out_ref[FIRST] = first_row.astype(F32)
    out_ref[BLK] = block.astype(F32)
    hot = pick - owned
    step = jnp.where(hot < 0, 0, jnp.where(hot < HOT, device_count - 1, 1))
    owner = (dest + step) & (device_count - 1)
    offset = owner ^ lax.axis_index("trade")
    scen_place = lax.axis_index("scen")
    ring = lax.shift_right_logical(offset, n_scen.bit_length() - 1)
    mine = ((offset & (n_scen - 1)) ^ ((ring & 1) * (n_scen // 2))) == scen_place
    slot = ring ^ (scen_place & (device_count // n_scen - 1) & 1)
    out_ref[SLOT] = jnp.where(mine, slot, -1).astype(F32)
    out_ref[PICK] = jnp.where(hot < HOT, pick, pick - HOT).astype(F32)

    maturity = (expiry.astype(F32) + frac_e + 1.0) * (4.0 / NE)
    moneyness = (strike.astype(F32) + frac_k - 0.5 * (NK - 1)) / NK
    scaled = notional * jnp.exp(-RATE * maturity)
    out_ref[ROOT] = jnp.sqrt(maturity)
    out_ref[MONEY] = moneyness
    out_ref[GROWTH] = jnp.exp(moneyness)
    out_ref[CASH] = scaled
    out_ref[VALUE] = scaled * forward

    strikes = lax.broadcasted_iota(jnp.int32, (NK, LANES), 0).astype(F32)
    expiries = lax.broadcasted_iota(jnp.int32, (2 * BAND, LANES), 0).astype(F32)

    def some(i, carry):
        for part in range(per_step):
            g = i * per_step + part
            columns = pl.ds(pl.multiple_of(g * LANES, LANES), LANES)
            taps = [out_ref[WE + tap, pl.ds(g, 1), :] for tap in range(4)]
            mix_ref[:, columns] = placed(
                expiries, taps, row_ref[0, pl.ds(g, 1), :], (2 * BAND, LANES)
            )
            taps = [tap_ref[tap, pl.ds(g, 1), :] for tap in range(4)]
            coef_ref[:, columns] = placed(strikes, taps, row_ref[1, pl.ds(g, 1), :], (NK, LANES))
        return carry

    lax.fori_loop(0, groups // per_step, some, 0)

    tiles = NE * NK // LANES
    in_tile = LANES // NK
    line = lax.broadcasted_iota(jnp.int32, (16, NE * NK), 0)
    for s in range(scenarios):
        copies[s].wait()
        wanted = jnp.where(line == (scen_ref[s] & 15), rows_ref[s].astype(F32), 0.0)
        wanted = jnp.sum(wanted, axis=0, keepdims=True)
        stacked = jnp.concatenate(
            [wanted[:, i * LANES : (i + 1) * LANES] for i in range(tiles)], axis=0
        )
        turned = jnp.transpose(stacked)
        for i in range(in_tile):
            wide_ref[s * NK : (s + 1) * NK, i * tiles : (i + 1) * tiles] = turned[
                i * NK : (i + 1) * NK, :
            ]
    matrix_ref[...] = wide_ref[...].astype(BF16)


def shift_kernel(per_step, matrix_ref, pre_ref, coef_ref, after_ref, shift_ref):
    scenarios, groups = shift_ref.shape[0], shift_ref.shape[1]
    tiles = NE * NK // LANES
    in_tile = LANES // NK
    shift = matrix_ref[...]
    place = lax.broadcasted_iota(jnp.int32, (NE, LANES), 0)
    expiries = (
        (place & (tiles - 1)) * in_tile + lax.shift_right_logical(place, tiles.bit_length() - 1)
    ).astype(F32)

    def some(i, carry):
        sides = []
        for part in range(per_step):
            g = i * per_step + part
            taps = [pre_ref[WE + tap, pl.ds(g, 1), :] for tap in range(4)]
            sides.append(
                placed(expiries, taps, pre_ref[FIRST, pl.ds(g, 1), :], (NE, LANES)).astype(BF16)
            )
        mixed = jnp.dot(shift, jnp.concatenate(sides, axis=1), preferred_element_type=F32)
        for part in range(per_step):
            g = i * per_step + part
            coefs = coef_ref[:, pl.ds(pl.multiple_of(g * LANES, LANES), LANES)]
            for s in range(scenarios):
                piece = mixed[s * NK : (s + 1) * NK, part * LANES : (part + 1) * LANES]
                shift_ref[s, pl.ds(g, 1), :] = jnp.sum(piece * coefs, axis=0, keepdims=True)
        return carry

    lax.fori_loop(0, groups // per_step, some, 0)


def surface_kernel(slot, owned, per_step, message_ref, pre_ref, mix_ref, coef_ref, *refs):
    before_ref = refs[0] if len(refs) == 5 else None
    out_ref, total_ref, table_ref, index_ref = refs[-4:]
    groups = pre_ref.shape[1]
    if before_ref is not None:
        total_ref[...] = before_ref[...].astype(F32)
    table_ref[0:WIDE, :] = message_ref[0:WIDE, :]
    table_ref[WIDE : WIDE + 3 * NK, :] = pltpu.roll(
        message_ref[0 : 3 * NK, :].astype(F32), (BLOCKS - 1) * owned, 1
    ).astype(BF16)
    extra = message_ref[WIDE : WIDE + EXTRA, 0 : 2 * LANES].astype(F32)
    betas = extra[0:1, 0:LANES] + extra[1:2, 0:LANES] + extra[2:3, 0:LANES]
    sub = 8
    for i in range(groups // sub):
        rows = pl.ds(i * sub, sub)
        held = pre_ref[SLOT, rows, :] == float(slot)
        local = pre_ref[PICK, rows, :]
        for h in range(HOT):
            hot = jnp.broadcast_to(extra[h : h + 1, LANES : 2 * LANES], (sub, LANES))
            local = jnp.where(local == float(owned + h), hot, local)
        looked = jnp.take_along_axis(
            jnp.broadcast_to(betas, (sub, LANES)),
            local.astype(jnp.int32),
            axis=1,
            mode="promise_in_bounds",
        )
        index_ref[rows, :] = jnp.where(held, local, -1.0)
        later = pl.ds(groups + i * sub, sub)
        other = 0.0 if before_ref is None else total_ref[later, :]
        total_ref[later, :] = jnp.where(held, looked, other)

    underlyings = lax.broadcasted_iota(jnp.int32, (owned, LANES), 0).astype(F32)
    zero = jnp.zeros((owned, LANES), BF16)

    def some(i, carry):
        sides = []
        for part in range(per_step):
            g = i * per_step + part
            index = jnp.broadcast_to(index_ref[pl.ds(g, 1), :], (owned, LANES))
            chosen = jnp.where(underlyings == index, 1.0, 0.0).astype(BF16)
            block = jnp.broadcast_to(pre_ref[BLK, pl.ds(g, 1), :], (owned, LANES)).astype(BF16)
            sides.append(
                jnp.concatenate(
                    [
                        jnp.where(block == jnp.asarray(j, BF16), chosen, zero)
                        for j in range(BLOCKS)
                    ],
                    axis=0,
                )
            )
        product = jnp.dot(
            table_ref[...], jnp.concatenate(sides, axis=1), preferred_element_type=F32
        )
        for part in range(per_step):
            g = i * per_step + part
            columns = slice(part * LANES, (part + 1) * LANES)
            here = pl.ds(pl.multiple_of(g * LANES, LANES), LANES)
            mix = mix_ref[:, here]
            curve = jnp.zeros((NK, LANES), F32)
            for a in range(REACH):
                curve = curve + product[a * NK : (a + 1) * NK, columns] * mix[a : a + 1, :]
            level = jnp.sum(curve * coef_ref[:, here], axis=0, keepdims=True)
            held = index_ref[pl.ds(g, 1), :] >= 0.0
            other = 0.0 if before_ref is None else total_ref[pl.ds(g, 1), :]
            total_ref[pl.ds(g, 1), :] = jnp.where(held, level, other)
        return carry

    lax.fori_loop(0, groups // per_step, some, 0)
    out_ref[...] = total_ref[...].astype(BF16)


def value_kernel(
    part_ref, rest_ref, shift_ref, pre_ref, price_ref, vega_ref, delta_ref, total_ref
):
    total_ref[...] = part_ref[...].astype(F32) + rest_ref[...].astype(F32)
    scenarios, groups = shift_ref.shape[0], shift_ref.shape[1]
    sub = 8
    for i in range(groups // sub):
        rows = pl.ds(i * sub, sub)
        later = pl.ds(groups + i * sub, sub)
        level = total_ref[rows, :] - pre_ref[BIAS, rows, :]
        slope = total_ref[later, :]
        root_time = pre_ref[ROOT, rows, :]
        moneyness = pre_ref[MONEY, rows, :]
        growth = pre_ref[GROWTH, rows, :]
        scaled = pre_ref[CASH, rows, :]
        value = pre_ref[VALUE, rows, :]
        results = ([], [], [])
        for s in range(scenarios):
            spread = jnp.exp(level + slope * shift_ref[s, rows, :]) * root_time
            upper_d = -moneyness / spread + 0.5 * spread
            lower_d = upper_d - spread
            cdf_upper = 0.5 + 0.5 * lax.erf(upper_d * INV_ROOT_TWO)
            cdf_lower = 0.5 + 0.5 * lax.erf(lower_d * INV_ROOT_TWO)
            results[0].append(value * (cdf_upper - growth * cdf_lower))
            results[1].append(value * INV_ROOT_TAU * jnp.exp(-0.5 * upper_d * upper_d) * root_time)
            results[2].append(scaled * cdf_upper)
        for r in range(sub):
            columns = pl.ds((i * sub + r) * LANES, LANES)
            for ref, result in zip((price_ref, vega_ref, delta_ref), results):
                ref[:, columns] = jnp.concatenate([x[r : r + 1, :] for x in result], axis=0)


def shards(
    log_vol,
    beta,
    shock_table,
    scen_ids,
    hot_index,
    dest,
    pick,
    expiry_cell,
    strike_cell,
    frac_e,
    frac_k,
    notional,
    forward,
):
    n_trade = lax.axis_size("trade")
    n_scen = lax.axis_size("scen")
    slots = n_trade // n_scen
    owned = log_vol.shape[0]
    trades = pick.shape[0]
    groups = trades // LANES
    scenarios = scen_ids.shape[0]

    message = pl.pallas_call(
        pack_kernel,
        out_shape=pltpu.VMEM((WIDE + EXTRA, BLOCKS * owned), BF16),
        in_specs=[HBM] * 3,
        out_specs=VMEM,
        scratch_shapes=[
            pltpu.VMEM(log_vol.shape, F32),
            pltpu.VMEM((1, owned), F32),
            pltpu.SMEM(hot_index.shape, jnp.int32),
            pltpu.SemaphoreType.DMA((BLOCKS * owned // LANES,)),
            pltpu.SemaphoreType.DMA((2,)),
        ],
        compiler_params=params(16384),
    )(*in_hbm(hot_index, log_vol, beta.reshape(1, owned)))

    received = [None] * slots
    for k in reversed(range(slots)):
        pairs = []
        for d in range(n_trade):
            for q in range(n_scen):
                ring = k ^ (q & (slots - 1) & 1)
                offset = ring * n_scen + (q ^ ((ring & 1) * (n_scen // 2)))
                pairs.append(((d ^ offset) * n_scen + q, d * n_scen + q))
        received[k] = lax.ppermute(message, ("trade", "scen"), pairs)

    dense = [
        column.reshape(groups, LANES)
        for column in (
            dest,
            pick,
            expiry_cell,
            strike_cell,
            frac_e,
            frac_k,
            notional,
            forward,
        )
    ]
    prepared, mix, coefs, matrix = pl.pallas_call(
        functools.partial(prepare_kernel, n_trade, n_scen, owned, PREPARE_STEP),
        out_shape=(
            pltpu.VMEM((PREPARED, groups, LANES), F32),
            pltpu.VMEM((2 * BAND, trades), F32),
            pltpu.VMEM((NK, trades), F32),
            pltpu.VMEM((scenarios * NK, NE), BF16),
        ),
        in_specs=[HBM] * 10,
        out_specs=(VMEM,) * 4,
        scratch_shapes=[
            pltpu.SMEM(scen_ids.shape, jnp.int32),
            pltpu.VMEM((4, groups, LANES), jnp.int32),
            pltpu.VMEM((4, groups, LANES), F32),
            pltpu.VMEM((scenarios, 16, NE * NK), BF16),
            pltpu.VMEM((scenarios * NK, NE), F32),
            pltpu.VMEM((2, groups, LANES), F32),
            pltpu.VMEM((4, groups, LANES), F32),
            pltpu.SemaphoreType.DMA((9,)),
            pltpu.SemaphoreType.DMA((scenarios,)),
        ],
        cost_estimate=pl.CostEstimate(flops=40_000_000, bytes_accessed=6_000_000, transcendentals=0),
        compiler_params=params(16384),
    )(*in_hbm(scen_ids, shock_table, *dense))

    partial_levels = None
    for k in reversed(range(slots)):
        before = [] if partial_levels is None else [partial_levels]
        partial_levels = pl.pallas_call(
            functools.partial(surface_kernel, k, owned, SURFACE_STEP),
            out_shape=jax.ShapeDtypeStruct((2 * groups, LANES), BF16),
            in_specs=[VMEM] * (4 + len(before)),
            out_specs=VMEM,
            scratch_shapes=[
                pltpu.VMEM((2 * groups, LANES), F32),
                pltpu.VMEM((WIDE + 3 * NK, BLOCKS * owned), BF16),
                pltpu.VMEM((groups, LANES), F32),
            ],
            compiler_params=params(32768),
        )(received[k], prepared, mix, coefs, *before)

    shift_level = pl.pallas_call(
        functools.partial(shift_kernel, SHIFT_STEP),
        out_shape=pltpu.VMEM((scenarios, groups, LANES), F32),
        in_specs=[VMEM] * 3 + [pl.BlockSpec(memory_space=pl.ANY)],
        out_specs=VMEM,
        cost_estimate=pl.CostEstimate(flops=40_000_000, bytes_accessed=2_000_000, transcendentals=0),
        compiler_params=params(16384),
    )(matrix, prepared, coefs, partial_levels)

    rest = jnp.zeros_like(partial_levels) if n_scen == 1 else None
    hop = n_scen // 2
    while hop:
        if rest is not None:
            partial_levels, shift_level = lax.optimization_barrier(
                (partial_levels + rest, shift_level)
            )
        rest = lax.ppermute(partial_levels, "scen", [(i, i ^ hop) for i in range(n_scen)])
        hop //= 2
    return pl.pallas_call(
        value_kernel,
        out_shape=(jax.ShapeDtypeStruct((scenarios, trades), F32),) * 3,
        in_specs=[VMEM] * 4,
        out_specs=(VMEM,) * 3,
        scratch_shapes=[pltpu.VMEM((2 * groups, LANES), F32)],
        compiler_params=params(8192),
    )(partial_levels, rest, shift_level, prepared)


def solution(mesh):
    in_specs = (
        P("trade", None),
        P("trade"),
        P(),
        P("scen"),
        P("trade"),
        P("trade", None),
        P("trade"),
        P("trade"),
        P("trade"),
        P("trade"),
        P("trade"),
        P("trade"),
        P("trade"),
    )
    out_specs = (P("scen", "trade"), P("scen", "trade"), P("scen", "trade"))
    return jax.shard_map(shards, mesh=mesh, in_specs=in_specs, out_specs=out_specs, check_vma=False)
```

```python
import functools

import jax
import jax.numpy as jnp
from jax import lax
from jax.experimental import pallas as pl
from jax.experimental.pallas import tpu as pltpu
from jax.sharding import PartitionSpec as P

NE = 64
NK = 32
HOT = 2
LANES = 128
BAND = 8
BLOCKS = NE // BAND
TILES = BAND * NK // LANES
WIDE = BAND * NK
REACH = BAND + 3
EXTRA = 16
CENTRE = 1.4
PREPARE_STEP = 8
SHIFT_STEP = 32
SURFACE_STEP = 64

RATE = 0.03
INV_ROOT_TWO = 0.7071067811865476
INV_ROOT_TAU = 0.3989422804014327

VMEM = pl.BlockSpec(memory_space=pltpu.VMEM)
HBM = pl.BlockSpec(memory_space=pltpu.HBM)
F32 = jnp.float32
BF16 = jnp.bfloat16

(WE, FIRST, BLK, SLOT, PICK, BIAS) = (0, 4, 5, 6, 7, 8)
(ROOT, MONEY, GROWTH, CASH, VALUE) = (9, 10, 11, 12, 13)
PREPARED = 14


def spline_weights(offset):
    square = offset * offset
    offset_cube = square * offset
    return (
        0.5 * (2.0 * square - offset_cube - offset),
        0.5 * (3.0 * offset_cube - 5.0 * square + 2.0),
        0.5 * (4.0 * square - 3.0 * offset_cube + offset),
        0.5 * (offset_cube - square),
    )


def in_hbm(*arrays):
    return [pltpu.with_memory_space_constraint(x, pltpu.HBM) if x.size > 1 else x for x in arrays]


def params(kilobytes):
    return pltpu.CompilerParams(vmem_limit_bytes=kilobytes << 10)


def pack_kernel(hot_in, log_vol_in, beta_in, out_ref, log_vol_ref, beta_ref, hot_ref, sems, small):
    owned = log_vol_ref.shape[0]
    per_tile = LANES // owned
    steps = BLOCKS // per_tile
    width = log_vol_ref.shape[1] // steps
    copies = []
    for tile in range(steps):
        columns = pl.ds(tile * width, width)
        copies.append(
            pltpu.make_async_copy(
                log_vol_in.at[:, columns], log_vol_ref.at[:, columns], sems.at[tile]
            )
        )
    copies.append(pltpu.make_async_copy(beta_in, beta_ref, small.at[0]))
    copies.append(pltpu.make_async_copy(hot_in, hot_ref, small.at[1]))
    for copy in copies:
        copy.start()
    for tile in range(steps):
        copies[tile].wait()
        for half in range(TILES):
            first = [((tile * per_tile + i) * TILES + half) * LANES for i in range(per_tile)]
            stacked = jnp.concatenate([log_vol_ref[:, c : c + LANES] for c in first], axis=0)
            out_ref[half * LANES : (half + 1) * LANES, tile * LANES : (tile + 1) * LANES] = (
                jnp.transpose(stacked) + CENTRE
            ).astype(BF16)
    copies[steps].wait()
    copies[steps + 1].wait()
    row = lax.broadcasted_iota(jnp.int32, (EXTRA, LANES), 0)
    beta = jnp.broadcast_to(beta_ref[...], (EXTRA, owned))
    high = beta.astype(BF16).astype(F32)
    middle = (beta - high).astype(BF16).astype(F32)
    low = beta - high - middle
    zero = jnp.zeros((EXTRA, LANES), F32)
    row_b = row[:, 0:owned]
    pieces = jnp.where(row_b == 0, high, jnp.where(row_b == 1, middle, jnp.where(row_b == 2, low, 0.0)))
    hots = zero
    for i in range(HOT):
        hots = jnp.where(row == i, hot_ref[i].astype(F32), hots)
    out_ref[WIDE : WIDE + EXTRA, 0:LANES] = zero.astype(BF16)
    out_ref[WIDE : WIDE + EXTRA, 0:owned] = pieces.astype(BF16)
    out_ref[WIDE : WIDE + EXTRA, LANES : 2 * LANES] = hots.astype(BF16)
    for tile in range(2, BLOCKS // per_tile):
        out_ref[WIDE : WIDE + EXTRA, tile * LANES : (tile + 1) * LANES] = zero.astype(BF16)


def placed(position, weights, first, shape):
    distance = position - jnp.broadcast_to(first, shape)
    result = jnp.zeros(shape, F32)
    for tap in range(4):
        result = jnp.where(distance == float(tap), jnp.broadcast_to(weights[tap], shape), result)
    return result


def prepare_kernel(
    device_count,
    n_scen,
    owned,
    per_step,
    scen_in,
    shock_ref,
    *refs,
):
    whole, reals = refs[:4], refs[4:8]
    out_ref, mix_ref, coef_ref, matrix_ref = refs[8:12]
    scen_ref, whole_ref, real_ref, rows_ref, wide_ref, row_ref, tap_ref, sems, sem = refs[12:]
    groups = out_ref.shape[1]
    scenarios = rows_ref.shape[0]
    ids = pltpu.make_async_copy(scen_in, scen_ref, sems.at[8])
    ids.start()
    columns = []
    for i in range(4):
        columns.append(pltpu.make_async_copy(whole[i], whole_ref.at[i], sems.at[i]))
        columns.append(pltpu.make_async_copy(reals[i], real_ref.at[i], sems.at[4 + i]))
    for copy in columns:
        copy.start()
    ids.wait()
    copies = []
    for s in range(scenarios):
        first = pl.multiple_of(lax.shift_right_logical(scen_ref[s], 4) * 16, 16)
        copies.append(
            pltpu.make_async_copy(shock_ref.at[pl.ds(first, 16), :], rows_ref.at[s], sem.at[s])
        )
        copies[-1].start()
    for copy in columns:
        copy.wait()
    dest, pick, expiry, strike = [whole_ref[i] for i in range(4)]
    frac_e, frac_k, notional, forward = [real_ref[i] for i in range(4)]
    weights = [w.astype(BF16).astype(F32) for w in spline_weights(frac_e)]
    for tap in range(4):
        out_ref[WE + tap] = weights[tap]
    taps = spline_weights(frac_k)
    for tap in range(4):
        tap_ref[tap] = taps[tap]
    out_ref[BIAS] = CENTRE * (
        (weights[0] + weights[1] + weights[2] + weights[3]) * (taps[0] + taps[1] + taps[2] + taps[3])
    )
    first_row = expiry - 1
    block = lax.shift_right_logical(first_row, BAND.bit_length() - 1)
    row_ref[0] = (first_row - block * BAND).astype(F32)
    row_ref[1] = (strike - 1).astype(F32)
    out_ref[FIRST] = first_row.astype(F32)
    out_ref[BLK] = block.astype(F32)
    hot = pick - owned
    step = jnp.where(hot < 0, 0, jnp.where(hot < HOT, device_count - 1, 1))
    owner = (dest + step) & (device_count - 1)
    offset = owner ^ lax.axis_index("trade")
    scen_place = lax.axis_index("scen")
    ring = lax.shift_right_logical(offset, n_scen.bit_length() - 1)
    mine = ((offset & (n_scen - 1)) ^ ((ring & 1) * (n_scen // 2))) == scen_place
    slot = ring ^ (scen_place & (device_count // n_scen - 1) & 1)
    out_ref[SLOT] = jnp.where(mine, slot, -1).astype(F32)
    out_ref[PICK] = jnp.where(hot < HOT, pick, pick - HOT).astype(F32)

    maturity = (expiry.astype(F32) + frac_e + 1.0) * (4.0 / NE)
    moneyness = (strike.astype(F32) + frac_k - 0.5 * (NK - 1)) / NK
    scaled = notional * jnp.exp(-RATE * maturity)
    out_ref[ROOT] = jnp.sqrt(maturity)
    out_ref[MONEY] = moneyness
    out_ref[GROWTH] = jnp.exp(moneyness)
    out_ref[CASH] = scaled
    out_ref[VALUE] = scaled * forward

    strikes = lax.broadcasted_iota(jnp.int32, (NK, LANES), 0).astype(F32)
    expiries = lax.broadcasted_iota(jnp.int32, (2 * BAND, LANES), 0).astype(F32)

    def some(i, carry):
        for part in range(per_step):
            g = i * per_step + part
            columns = pl.ds(pl.multiple_of(g * LANES, LANES), LANES)
            taps = [out_ref[WE + tap, pl.ds(g, 1), :] for tap in range(4)]
            mix_ref[:, columns] = placed(
                expiries, taps, row_ref[0, pl.ds(g, 1), :], (2 * BAND, LANES)
            )
            taps = [tap_ref[tap, pl.ds(g, 1), :] for tap in range(4)]
            coef_ref[:, columns] = placed(strikes, taps, row_ref[1, pl.ds(g, 1), :], (NK, LANES))
        return carry

    lax.fori_loop(0, groups // per_step, some, 0)

    tiles = NE * NK // LANES
    in_tile = LANES // NK
    line = lax.broadcasted_iota(jnp.int32, (16, NE * NK), 0)
    for s in range(scenarios):
        copies[s].wait()
        wanted = jnp.where(line == (scen_ref[s] & 15), rows_ref[s].astype(F32), 0.0)
        wanted = jnp.sum(wanted, axis=0, keepdims=True)
        stacked = jnp.concatenate(
            [wanted[:, i * LANES : (i + 1) * LANES] for i in range(tiles)], axis=0
        )
        turned = jnp.transpose(stacked)
        for i in range(in_tile):
            wide_ref[s * NK : (s + 1) * NK, i * tiles : (i + 1) * tiles] = turned[
                i * NK : (i + 1) * NK, :
            ]
    matrix_ref[...] = wide_ref[...].astype(BF16)


def shift_kernel(per_step, matrix_ref, pre_ref, coef_ref, after_ref, shift_ref):
    scenarios, groups = shift_ref.shape[0], shift_ref.shape[1]
    tiles = NE * NK // LANES
    in_tile = LANES // NK
    shift = matrix_ref[...]
    place = lax.broadcasted_iota(jnp.int32, (NE, LANES), 0)
    expiries = (
        (place & (tiles - 1)) * in_tile + lax.shift_right_logical(place, tiles.bit_length() - 1)
    ).astype(F32)

    def some(i, carry):
        sides = []
        for part in range(per_step):
            g = i * per_step + part
            taps = [pre_ref[WE + tap, pl.ds(g, 1), :] for tap in range(4)]
            sides.append(
                placed(expiries, taps, pre_ref[FIRST, pl.ds(g, 1), :], (NE, LANES)).astype(BF16)
            )
        mixed = jnp.dot(shift, jnp.concatenate(sides, axis=1), preferred_element_type=F32)
        for part in range(per_step):
            g = i * per_step + part
            coefs = coef_ref[:, pl.ds(pl.multiple_of(g * LANES, LANES), LANES)]
            for s in range(scenarios):
                piece = mixed[s * NK : (s + 1) * NK, part * LANES : (part + 1) * LANES]
                shift_ref[s, pl.ds(g, 1), :] = jnp.sum(piece * coefs, axis=0, keepdims=True)
        return carry

    lax.fori_loop(0, groups // per_step, some, 0)


def surface_kernel(slot, owned, per_step, message_ref, pre_ref, mix_ref, coef_ref, *refs):
    before_ref = refs[0] if len(refs) == 5 else None
    out_ref, total_ref, table_ref, index_ref = refs[-4:]
    groups = pre_ref.shape[1]
    if before_ref is not None:
        total_ref[...] = before_ref[...].astype(F32)
    table_ref[0:WIDE, :] = message_ref[0:WIDE, :]
    table_ref[WIDE : WIDE + 3 * NK, :] = pltpu.roll(
        message_ref[0 : 3 * NK, :].astype(F32), (BLOCKS - 1) * owned, 1
    ).astype(BF16)
    extra = message_ref[WIDE : WIDE + EXTRA, 0 : 2 * LANES].astype(F32)
    betas = extra[0:1, 0:LANES] + extra[1:2, 0:LANES] + extra[2:3, 0:LANES]
    sub = 8
    for i in range(groups // sub):
        rows = pl.ds(i * sub, sub)
        held = pre_ref[SLOT, rows, :] == float(slot)
        local = pre_ref[PICK, rows, :]
        for h in range(HOT):
            hot = jnp.broadcast_to(extra[h : h + 1, LANES : 2 * LANES], (sub, LANES))
            local = jnp.where(local == float(owned + h), hot, local)
        looked = jnp.take_along_axis(
            jnp.broadcast_to(betas, (sub, LANES)),
            local.astype(jnp.int32),
            axis=1,
            mode="promise_in_bounds",
        )
        index_ref[rows, :] = jnp.where(held, local, -1.0)
        later = pl.ds(groups + i * sub, sub)
        other = 0.0 if before_ref is None else total_ref[later, :]
        total_ref[later, :] = jnp.where(held, looked, other)

    underlyings = lax.broadcasted_iota(jnp.int32, (owned, LANES), 0).astype(F32)
    zero = jnp.zeros((owned, LANES), BF16)

    def some(i, carry):
        sides = []
        for part in range(per_step):
            g = i * per_step + part
            index = jnp.broadcast_to(index_ref[pl.ds(g, 1), :], (owned, LANES))
            chosen = jnp.where(underlyings == index, 1.0, 0.0).astype(BF16)
            block = jnp.broadcast_to(pre_ref[BLK, pl.ds(g, 1), :], (owned, LANES)).astype(BF16)
            sides.append(
                jnp.concatenate(
                    [
                        jnp.where(block == jnp.asarray(j, BF16), chosen, zero)
                        for j in range(BLOCKS)
                    ],
                    axis=0,
                )
            )
        product = jnp.dot(
            table_ref[...], jnp.concatenate(sides, axis=1), preferred_element_type=F32
        )
        for part in range(per_step):
            g = i * per_step + part
            columns = slice(part * LANES, (part + 1) * LANES)
            here = pl.ds(pl.multiple_of(g * LANES, LANES), LANES)
            mix = mix_ref[:, here]
            curve = jnp.zeros((NK, LANES), F32)
            for a in range(REACH):
                curve = curve + product[a * NK : (a + 1) * NK, columns] * mix[a : a + 1, :]
            level = jnp.sum(curve * coef_ref[:, here], axis=0, keepdims=True)
            held = index_ref[pl.ds(g, 1), :] >= 0.0
            other = 0.0 if before_ref is None else total_ref[pl.ds(g, 1), :]
            total_ref[pl.ds(g, 1), :] = jnp.where(held, level, other)
        return carry

    lax.fori_loop(0, groups // per_step, some, 0)
    out_ref[...] = total_ref[...].astype(BF16)


def value_kernel(
    part_ref, rest_ref, shift_ref, pre_ref, price_ref, vega_ref, delta_ref, total_ref
):
    total_ref[...] = part_ref[...].astype(F32) + rest_ref[...].astype(F32)
    scenarios, groups = shift_ref.shape[0], shift_ref.shape[1]
    sub = 8
    for i in range(groups // sub):
        rows = pl.ds(i * sub, sub)
        later = pl.ds(groups + i * sub, sub)
        level = total_ref[rows, :] - pre_ref[BIAS, rows, :]
        slope = total_ref[later, :]
        root_time = pre_ref[ROOT, rows, :]
        moneyness = pre_ref[MONEY, rows, :]
        growth = pre_ref[GROWTH, rows, :]
        scaled = pre_ref[CASH, rows, :]
        value = pre_ref[VALUE, rows, :]
        results = ([], [], [])
        for s in range(scenarios):
            spread = jnp.exp(level + slope * shift_ref[s, rows, :]) * root_time
            upper_d = -moneyness / spread + 0.5 * spread
            lower_d = upper_d - spread
            cdf_upper = 0.5 + 0.5 * lax.erf(upper_d * INV_ROOT_TWO)
            cdf_lower = 0.5 + 0.5 * lax.erf(lower_d * INV_ROOT_TWO)
            results[0].append(value * (cdf_upper - growth * cdf_lower))
            results[1].append(value * INV_ROOT_TAU * jnp.exp(-0.5 * upper_d * upper_d) * root_time)
            results[2].append(scaled * cdf_upper)
        for r in range(sub):
            columns = pl.ds((i * sub + r) * LANES, LANES)
            for ref, result in zip((price_ref, vega_ref, delta_ref), results):
                ref[:, columns] = jnp.concatenate([x[r : r + 1, :] for x in result], axis=0)


def shards(
    log_vol,
    beta,
    shock_table,
    scen_ids,
    hot_index,
    dest,
    pick,
    expiry_cell,
    strike_cell,
    frac_e,
    frac_k,
    notional,
    forward,
):
    n_trade = lax.axis_size("trade")
    n_scen = lax.axis_size("scen")
    slots = n_trade // n_scen
    owned = log_vol.shape[0]
    trades = pick.shape[0]
    groups = trades // LANES
    scenarios = scen_ids.shape[0]

    message = pl.pallas_call(
        pack_kernel,
        out_shape=pltpu.VMEM((WIDE + EXTRA, BLOCKS * owned), BF16),
        in_specs=[HBM] * 3,
        out_specs=VMEM,
        scratch_shapes=[
            pltpu.VMEM(log_vol.shape, F32),
            pltpu.VMEM((1, owned), F32),
            pltpu.SMEM(hot_index.shape, jnp.int32),
            pltpu.SemaphoreType.DMA((BLOCKS * owned // LANES,)),
            pltpu.SemaphoreType.DMA((2,)),
        ],
        compiler_params=params(16384),
    )(*in_hbm(hot_index, log_vol, beta.reshape(1, owned)))

    received = [None] * slots
    for k in reversed(range(slots)):
        pairs = []
        for d in range(n_trade):
            for q in range(n_scen):
                ring = k ^ (q & (slots - 1) & 1)
                offset = ring * n_scen + (q ^ ((ring & 1) * (n_scen // 2)))
                pairs.append(((d ^ offset) * n_scen + q, d * n_scen + q))
        received[k] = lax.ppermute(message, ("trade", "scen"), pairs)

    dense = [
        column.reshape(groups, LANES)
        for column in (
            dest,
            pick,
            expiry_cell,
            strike_cell,
            frac_e,
            frac_k,
            notional,
            forward,
        )
    ]
    prepared, mix, coefs, matrix = pl.pallas_call(
        functools.partial(prepare_kernel, n_trade, n_scen, owned, PREPARE_STEP),
        out_shape=(
            pltpu.VMEM((PREPARED, groups, LANES), F32),
            pltpu.VMEM((2 * BAND, trades), F32),
            pltpu.VMEM((NK, trades), F32),
            pltpu.VMEM((scenarios * NK, NE), BF16),
        ),
        in_specs=[HBM] * 10,
        out_specs=(VMEM,) * 4,
        scratch_shapes=[
            pltpu.SMEM(scen_ids.shape, jnp.int32),
            pltpu.VMEM((4, groups, LANES), jnp.int32),
            pltpu.VMEM((4, groups, LANES), F32),
            pltpu.VMEM((scenarios, 16, NE * NK), BF16),
            pltpu.VMEM((scenarios * NK, NE), F32),
            pltpu.VMEM((2, groups, LANES), F32),
            pltpu.VMEM((4, groups, LANES), F32),
            pltpu.SemaphoreType.DMA((9,)),
            pltpu.SemaphoreType.DMA((scenarios,)),
        ],
        cost_estimate=pl.CostEstimate(flops=40_000_000, bytes_accessed=6_000_000, transcendentals=0),
        compiler_params=params(16384),
    )(*in_hbm(scen_ids, shock_table, *dense))

    partial_levels = None
    for k in reversed(range(slots)):
        before = [] if partial_levels is None else [partial_levels]
        partial_levels = pl.pallas_call(
            functools.partial(surface_kernel, k, owned, SURFACE_STEP),
            out_shape=jax.ShapeDtypeStruct((2 * groups, LANES), BF16),
            in_specs=[VMEM] * (4 + len(before)),
            out_specs=VMEM,
            scratch_shapes=[
                pltpu.VMEM((2 * groups, LANES), F32),
                pltpu.VMEM((WIDE + 3 * NK, BLOCKS * owned), BF16),
                pltpu.VMEM((groups, LANES), F32),
            ],
            compiler_params=params(32768),
        )(received[k], prepared, mix, coefs, *before)

    shift_level = pl.pallas_call(
        functools.partial(shift_kernel, SHIFT_STEP),
        out_shape=pltpu.VMEM((scenarios, groups, LANES), F32),
        in_specs=[VMEM] * 3 + [pl.BlockSpec(memory_space=pl.ANY)],
        out_specs=VMEM,
        cost_estimate=pl.CostEstimate(flops=40_000_000, bytes_accessed=2_000_000, transcendentals=0),
        compiler_params=params(16384),
    )(matrix, prepared, coefs, partial_levels)

    rest = jnp.zeros_like(partial_levels) if n_scen == 1 else None
    hop = 1
    while hop < n_scen:
        if rest is not None:
            partial_levels = partial_levels + rest
        rest = lax.ppermute(partial_levels, "scen", [(i, i ^ hop) for i in range(n_scen)])
        hop *= 2
    return pl.pallas_call(
        value_kernel,
        out_shape=(jax.ShapeDtypeStruct((scenarios, trades), F32),) * 3,
        in_specs=[VMEM] * 4,
        out_specs=(VMEM,) * 3,
        scratch_shapes=[pltpu.VMEM((2 * groups, LANES), F32)],
        compiler_params=params(8192),
    )(partial_levels, rest, shift_level, prepared)


def solution(mesh):
    in_specs = (
        P("trade", None),
        P("trade"),
        P(),
        P("scen"),
        P("trade"),
        P("trade", None),
        P("trade"),
        P("trade"),
        P("trade"),
        P("trade"),
        P("trade"),
        P("trade"),
        P("trade"),
    )
    out_specs = (P("scen", "trade"), P("scen", "trade"), P("scen", "trade"))
    return jax.shard_map(shards, mesh=mesh, in_specs=in_specs, out_specs=out_specs, check_vma=False)
```

```python
import functools

import jax
import jax.numpy as jnp
from jax import lax
from jax.experimental import pallas as pl
from jax.experimental.pallas import tpu as pltpu
from jax.sharding import PartitionSpec as P

NE = 64
NK = 32
HOT = 2
LANES = 128
BAND = 8
BLOCKS = NE // BAND
TILES = BAND * NK // LANES
WIDE = BAND * NK
REACH = BAND + 3
EXTRA = 16
CENTRE = 1.4
PREPARE_STEP = 8
SHIFT_STEP = 32
SURFACE_STEP = 64

RATE = 0.03
INV_ROOT_TWO = 0.7071067811865476
INV_ROOT_TAU = 0.3989422804014327

VMEM = pl.BlockSpec(memory_space=pltpu.VMEM)
HBM = pl.BlockSpec(memory_space=pltpu.HBM)
F32 = jnp.float32
BF16 = jnp.bfloat16

(WE, FIRST, BLK, SLOT, PICK, BIAS) = (0, 4, 5, 6, 7, 8)
(ROOT, MONEY, GROWTH, CASH, VALUE) = (9, 10, 11, 12, 13)
PREPARED = 14


def spline_weights(offset):
    square = offset * offset
    offset_cube = square * offset
    return (
        0.5 * (2.0 * square - offset_cube - offset),
        0.5 * (3.0 * offset_cube - 5.0 * square + 2.0),
        0.5 * (4.0 * square - 3.0 * offset_cube + offset),
        0.5 * (offset_cube - square),
    )


def in_hbm(*arrays):
    return [pltpu.with_memory_space_constraint(x, pltpu.HBM) if x.size > 1 else x for x in arrays]


def params(kilobytes):
    return pltpu.CompilerParams(vmem_limit_bytes=kilobytes << 10)


def pack_kernel(hot_in, log_vol_in, beta_in, out_ref, log_vol_ref, beta_ref, hot_ref, sems, small):
    owned = log_vol_ref.shape[0]
    per_tile = LANES // owned
    steps = BLOCKS // per_tile
    width = log_vol_ref.shape[1] // steps
    copies = []
    for tile in range(steps):
        columns = pl.ds(tile * width, width)
        copies.append(
            pltpu.make_async_copy(
                log_vol_in.at[:, columns], log_vol_ref.at[:, columns], sems.at[tile]
            )
        )
    copies.append(pltpu.make_async_copy(beta_in, beta_ref, small.at[0]))
    copies.append(pltpu.make_async_copy(hot_in, hot_ref, small.at[1]))
    for copy in copies:
        copy.start()
    for tile in range(steps):
        copies[tile].wait()
        for half in range(TILES):
            first = [((tile * per_tile + i) * TILES + half) * LANES for i in range(per_tile)]
            stacked = jnp.concatenate([log_vol_ref[:, c : c + LANES] for c in first], axis=0)
            out_ref[half * LANES : (half + 1) * LANES, tile * LANES : (tile + 1) * LANES] = (
                jnp.transpose(stacked) + CENTRE
            ).astype(BF16)
    copies[steps].wait()
    copies[steps + 1].wait()
    row = lax.broadcasted_iota(jnp.int32, (EXTRA, LANES), 0)
    beta = jnp.broadcast_to(beta_ref[...], (EXTRA, owned))
    high = beta.astype(BF16).astype(F32)
    middle = (beta - high).astype(BF16).astype(F32)
    low = beta - high - middle
    zero = jnp.zeros((EXTRA, LANES), F32)
    row_b = row[:, 0:owned]
    pieces = jnp.where(row_b == 0, high, jnp.where(row_b == 1, middle, jnp.where(row_b == 2, low, 0.0)))
    hots = zero
    for i in range(HOT):
        hots = jnp.where(row == i, hot_ref[i].astype(F32), hots)
    out_ref[WIDE : WIDE + EXTRA, 0:LANES] = zero.astype(BF16)
    out_ref[WIDE : WIDE + EXTRA, 0:owned] = pieces.astype(BF16)
    out_ref[WIDE : WIDE + EXTRA, LANES : 2 * LANES] = hots.astype(BF16)
    for tile in range(2, BLOCKS // per_tile):
        out_ref[WIDE : WIDE + EXTRA, tile * LANES : (tile + 1) * LANES] = zero.astype(BF16)


def placed(position, weights, first, shape):
    distance = position - jnp.broadcast_to(first, shape)
    result = jnp.zeros(shape, F32)
    for tap in range(4):
        result = jnp.where(distance == float(tap), jnp.broadcast_to(weights[tap], shape), result)
    return result


def parity(value, count):
    return sum((value >> i) & 1 for i in range(count.bit_length() - 1)) & 1


def prepare_kernel(
    device_count,
    n_scen,
    owned,
    per_step,
    scen_in,
    shock_ref,
    *refs,
):
    whole, reals = refs[:4], refs[4:8]
    out_ref, mix_ref, coef_ref, matrix_ref = refs[8:12]
    scen_ref, whole_ref, real_ref, rows_ref, wide_ref, row_ref, tap_ref, sems, sem = refs[12:]
    groups = out_ref.shape[1]
    scenarios = rows_ref.shape[0]
    ids = pltpu.make_async_copy(scen_in, scen_ref, sems.at[8])
    ids.start()
    columns = []
    for i in range(4):
        columns.append(pltpu.make_async_copy(whole[i], whole_ref.at[i], sems.at[i]))
        columns.append(pltpu.make_async_copy(reals[i], real_ref.at[i], sems.at[4 + i]))
    for copy in columns:
        copy.start()
    ids.wait()
    copies = []
    for s in range(scenarios):
        first = pl.multiple_of(lax.shift_right_logical(scen_ref[s], 4) * 16, 16)
        copies.append(
            pltpu.make_async_copy(shock_ref.at[pl.ds(first, 16), :], rows_ref.at[s], sem.at[s])
        )
        copies[-1].start()
    for copy in columns:
        copy.wait()
    dest, pick, expiry, strike = [whole_ref[i] for i in range(4)]
    frac_e, frac_k, notional, forward = [real_ref[i] for i in range(4)]
    weights = [w.astype(BF16).astype(F32) for w in spline_weights(frac_e)]
    for tap in range(4):
        out_ref[WE + tap] = weights[tap]
    taps = spline_weights(frac_k)
    for tap in range(4):
        tap_ref[tap] = taps[tap]
    out_ref[BIAS] = CENTRE * (
        (weights[0] + weights[1] + weights[2] + weights[3]) * (taps[0] + taps[1] + taps[2] + taps[3])
    )
    first_row = expiry - 1
    block = lax.shift_right_logical(first_row, BAND.bit_length() - 1)
    row_ref[0] = (first_row - block * BAND).astype(F32)
    row_ref[1] = (strike - 1).astype(F32)
    out_ref[FIRST] = first_row.astype(F32)
    out_ref[BLK] = block.astype(F32)
    hot = pick - owned
    step = jnp.where(hot < 0, 0, jnp.where(hot < HOT, device_count - 1, 1))
    owner = (dest + step) & (device_count - 1)
    offset = owner ^ lax.axis_index("trade")
    scen_place = lax.axis_index("scen")
    ring = lax.shift_right_logical(offset, n_scen.bit_length() - 1)
    mine = ((offset & (n_scen - 1)) ^ ((ring & 1) * (n_scen // 2))) == scen_place
    slot = ring ^ (parity(scen_place, n_scen) & (device_count // n_scen - 1))
    out_ref[SLOT] = jnp.where(mine, slot, -1).astype(F32)
    out_ref[PICK] = jnp.where(hot < HOT, pick, pick - HOT).astype(F32)

    maturity = (expiry.astype(F32) + frac_e + 1.0) * (4.0 / NE)
    moneyness = (strike.astype(F32) + frac_k - 0.5 * (NK - 1)) / NK
    scaled = notional * jnp.exp(-RATE * maturity)
    out_ref[ROOT] = jnp.sqrt(maturity)
    out_ref[MONEY] = moneyness
    out_ref[GROWTH] = jnp.exp(moneyness)
    out_ref[CASH] = scaled
    out_ref[VALUE] = scaled * forward

    strikes = lax.broadcasted_iota(jnp.int32, (NK, LANES), 0).astype(F32)
    expiries = lax.broadcasted_iota(jnp.int32, (2 * BAND, LANES), 0).astype(F32)

    def some(i, carry):
        for part in range(per_step):
            g = i * per_step + part
            columns = pl.ds(pl.multiple_of(g * LANES, LANES), LANES)
            taps = [out_ref[WE + tap, pl.ds(g, 1), :] for tap in range(4)]
            mix_ref[:, columns] = placed(
                expiries, taps, row_ref[0, pl.ds(g, 1), :], (2 * BAND, LANES)
            )
            taps = [tap_ref[tap, pl.ds(g, 1), :] for tap in range(4)]
            coef_ref[:, columns] = placed(strikes, taps, row_ref[1, pl.ds(g, 1), :], (NK, LANES))
        return carry

    lax.fori_loop(0, groups // per_step, some, 0)

    tiles = NE * NK // LANES
    in_tile = LANES // NK
    line = lax.broadcasted_iota(jnp.int32, (16, NE * NK), 0)
    for s in range(scenarios):
        copies[s].wait()
        wanted = jnp.where(line == (scen_ref[s] & 15), rows_ref[s].astype(F32), 0.0)
        wanted = jnp.sum(wanted, axis=0, keepdims=True)
        stacked = jnp.concatenate(
            [wanted[:, i * LANES : (i + 1) * LANES] for i in range(tiles)], axis=0
        )
        turned = jnp.transpose(stacked)
        for i in range(in_tile):
            wide_ref[s * NK : (s + 1) * NK, i * tiles : (i + 1) * tiles] = turned[
                i * NK : (i + 1) * NK, :
            ]
    matrix_ref[...] = wide_ref[...].astype(BF16)


def shift_kernel(per_step, matrix_ref, pre_ref, coef_ref, after_ref, shift_ref):
    scenarios, groups = shift_ref.shape[0], shift_ref.shape[1]
    tiles = NE * NK // LANES
    in_tile = LANES // NK
    shift = matrix_ref[...]
    place = lax.broadcasted_iota(jnp.int32, (NE, LANES), 0)
    expiries = (
        (place & (tiles - 1)) * in_tile + lax.shift_right_logical(place, tiles.bit_length() - 1)
    ).astype(F32)

    def some(i, carry):
        sides = []
        for part in range(per_step):
            g = i * per_step + part
            taps = [pre_ref[WE + tap, pl.ds(g, 1), :] for tap in range(4)]
            sides.append(
                placed(expiries, taps, pre_ref[FIRST, pl.ds(g, 1), :], (NE, LANES)).astype(BF16)
            )
        mixed = jnp.dot(shift, jnp.concatenate(sides, axis=1), preferred_element_type=F32)
        for part in range(per_step):
            g = i * per_step + part
            coefs = coef_ref[:, pl.ds(pl.multiple_of(g * LANES, LANES), LANES)]
            for s in range(scenarios):
                piece = mixed[s * NK : (s + 1) * NK, part * LANES : (part + 1) * LANES]
                shift_ref[s, pl.ds(g, 1), :] = jnp.sum(piece * coefs, axis=0, keepdims=True)
        return carry

    lax.fori_loop(0, groups // per_step, some, 0)


def surface_kernel(slot, owned, per_step, message_ref, pre_ref, mix_ref, coef_ref, *refs):
    before_ref = refs[0] if len(refs) == 5 else None
    out_ref, total_ref, table_ref, index_ref = refs[-4:]
    groups = pre_ref.shape[1]
    if before_ref is not None:
        total_ref[...] = before_ref[...].astype(F32)
    table_ref[0:WIDE, :] = message_ref[0:WIDE, :]
    table_ref[WIDE : WIDE + 3 * NK, :] = pltpu.roll(
        message_ref[0 : 3 * NK, :].astype(F32), (BLOCKS - 1) * owned, 1
    ).astype(BF16)
    extra = message_ref[WIDE : WIDE + EXTRA, 0 : 2 * LANES].astype(F32)
    betas = extra[0:1, 0:LANES] + extra[1:2, 0:LANES] + extra[2:3, 0:LANES]
    sub = 8
    for i in range(groups // sub):
        rows = pl.ds(i * sub, sub)
        held = pre_ref[SLOT, rows, :] == float(slot)
        local = pre_ref[PICK, rows, :]
        for h in range(HOT):
            hot = jnp.broadcast_to(extra[h : h + 1, LANES : 2 * LANES], (sub, LANES))
            local = jnp.where(local == float(owned + h), hot, local)
        looked = jnp.take_along_axis(
            jnp.broadcast_to(betas, (sub, LANES)),
            local.astype(jnp.int32),
            axis=1,
            mode="promise_in_bounds",
        )
        index_ref[rows, :] = jnp.where(held, local, -1.0)
        later = pl.ds(groups + i * sub, sub)
        other = 0.0 if before_ref is None else total_ref[later, :]
        total_ref[later, :] = jnp.where(held, looked, other)

    underlyings = lax.broadcasted_iota(jnp.int32, (owned, LANES), 0).astype(F32)
    zero = jnp.zeros((owned, LANES), BF16)

    def some(i, carry):
        sides = []
        for part in range(per_step):
            g = i * per_step + part
            index = jnp.broadcast_to(index_ref[pl.ds(g, 1), :], (owned, LANES))
            chosen = jnp.where(underlyings == index, 1.0, 0.0).astype(BF16)
            block = jnp.broadcast_to(pre_ref[BLK, pl.ds(g, 1), :], (owned, LANES)).astype(BF16)
            sides.append(
                jnp.concatenate(
                    [
                        jnp.where(block == jnp.asarray(j, BF16), chosen, zero)
                        for j in range(BLOCKS)
                    ],
                    axis=0,
                )
            )
        product = jnp.dot(
            table_ref[...], jnp.concatenate(sides, axis=1), preferred_element_type=F32
        )
        for part in range(per_step):
            g = i * per_step + part
            columns = slice(part * LANES, (part + 1) * LANES)
            here = pl.ds(pl.multiple_of(g * LANES, LANES), LANES)
            mix = mix_ref[:, here]
            curve = jnp.zeros((NK, LANES), F32)
            for a in range(REACH):
                curve = curve + product[a * NK : (a + 1) * NK, columns] * mix[a : a + 1, :]
            level = jnp.sum(curve * coef_ref[:, here], axis=0, keepdims=True)
            held = index_ref[pl.ds(g, 1), :] >= 0.0
            other = 0.0 if before_ref is None else total_ref[pl.ds(g, 1), :]
            total_ref[pl.ds(g, 1), :] = jnp.where(held, level, other)
        return carry

    lax.fori_loop(0, groups // per_step, some, 0)
    out_ref[...] = total_ref[...].astype(BF16)


def value_kernel(
    part_ref, rest_ref, shift_ref, pre_ref, price_ref, vega_ref, delta_ref, total_ref
):
    total_ref[...] = part_ref[...].astype(F32) + rest_ref[...].astype(F32)
    scenarios, groups = shift_ref.shape[0], shift_ref.shape[1]
    sub = 8
    for i in range(groups // sub):
        rows = pl.ds(i * sub, sub)
        later = pl.ds(groups + i * sub, sub)
        level = total_ref[rows, :] - pre_ref[BIAS, rows, :]
        slope = total_ref[later, :]
        root_time = pre_ref[ROOT, rows, :]
        moneyness = pre_ref[MONEY, rows, :]
        growth = pre_ref[GROWTH, rows, :]
        scaled = pre_ref[CASH, rows, :]
        value = pre_ref[VALUE, rows, :]
        results = ([], [], [])
        for s in range(scenarios):
            spread = jnp.exp(level + slope * shift_ref[s, rows, :]) * root_time
            upper_d = -moneyness / spread + 0.5 * spread
            lower_d = upper_d - spread
            cdf_upper = 0.5 + 0.5 * lax.erf(upper_d * INV_ROOT_TWO)
            cdf_lower = 0.5 + 0.5 * lax.erf(lower_d * INV_ROOT_TWO)
            results[0].append(value * (cdf_upper - growth * cdf_lower))
            results[1].append(value * INV_ROOT_TAU * jnp.exp(-0.5 * upper_d * upper_d) * root_time)
            results[2].append(scaled * cdf_upper)
        for r in range(sub):
            columns = pl.ds((i * sub + r) * LANES, LANES)
            for ref, result in zip((price_ref, vega_ref, delta_ref), results):
                ref[:, columns] = jnp.concatenate([x[r : r + 1, :] for x in result], axis=0)


def shards(
    log_vol,
    beta,
    shock_table,
    scen_ids,
    hot_index,
    dest,
    pick,
    expiry_cell,
    strike_cell,
    frac_e,
    frac_k,
    notional,
    forward,
):
    n_trade = lax.axis_size("trade")
    n_scen = lax.axis_size("scen")
    slots = n_trade // n_scen
    owned = log_vol.shape[0]
    trades = pick.shape[0]
    groups = trades // LANES
    scenarios = scen_ids.shape[0]

    message = pl.pallas_call(
        pack_kernel,
        out_shape=pltpu.VMEM((WIDE + EXTRA, BLOCKS * owned), BF16),
        in_specs=[HBM] * 3,
        out_specs=VMEM,
        scratch_shapes=[
            pltpu.VMEM(log_vol.shape, F32),
            pltpu.VMEM((1, owned), F32),
            pltpu.SMEM(hot_index.shape, jnp.int32),
            pltpu.SemaphoreType.DMA((BLOCKS * owned // LANES,)),
            pltpu.SemaphoreType.DMA((2,)),
        ],
        compiler_params=params(16384),
    )(*in_hbm(hot_index, log_vol, beta.reshape(1, owned)))

    received = [None] * slots
    for k in reversed(range(slots)):
        pairs = []
        for d in range(n_trade):
            for q in range(n_scen):
                ring = k ^ (parity(q, n_scen) & (slots - 1))
                offset = ring * n_scen + (q ^ ((ring & 1) * (n_scen // 2)))
                pairs.append(((d ^ offset) * n_scen + q, d * n_scen + q))
        received[k] = lax.ppermute(message, ("trade", "scen"), pairs)

    dense = [
        column.reshape(groups, LANES)
        for column in (
            dest,
            pick,
            expiry_cell,
            strike_cell,
            frac_e,
            frac_k,
            notional,
            forward,
        )
    ]
    prepared, mix, coefs, matrix = pl.pallas_call(
        functools.partial(prepare_kernel, n_trade, n_scen, owned, PREPARE_STEP),
        out_shape=(
            pltpu.VMEM((PREPARED, groups, LANES), F32),
            pltpu.VMEM((2 * BAND, trades), F32),
            pltpu.VMEM((NK, trades), F32),
            pltpu.VMEM((scenarios * NK, NE), BF16),
        ),
        in_specs=[HBM] * 10,
        out_specs=(VMEM,) * 4,
        scratch_shapes=[
            pltpu.SMEM(scen_ids.shape, jnp.int32),
            pltpu.VMEM((4, groups, LANES), jnp.int32),
            pltpu.VMEM((4, groups, LANES), F32),
            pltpu.VMEM((scenarios, 16, NE * NK), BF16),
            pltpu.VMEM((scenarios * NK, NE), F32),
            pltpu.VMEM((2, groups, LANES), F32),
            pltpu.VMEM((4, groups, LANES), F32),
            pltpu.SemaphoreType.DMA((9,)),
            pltpu.SemaphoreType.DMA((scenarios,)),
        ],
        cost_estimate=pl.CostEstimate(flops=40_000_000, bytes_accessed=6_000_000, transcendentals=0),
        compiler_params=params(16384),
    )(*in_hbm(scen_ids, shock_table, *dense))

    partial_levels = None
    for k in reversed(range(slots)):
        before = [] if partial_levels is None else [partial_levels]
        partial_levels = pl.pallas_call(
            functools.partial(surface_kernel, k, owned, SURFACE_STEP),
            out_shape=jax.ShapeDtypeStruct((2 * groups, LANES), BF16),
            in_specs=[VMEM] * (4 + len(before)),
            out_specs=VMEM,
            scratch_shapes=[
                pltpu.VMEM((2 * groups, LANES), F32),
                pltpu.VMEM((WIDE + 3 * NK, BLOCKS * owned), BF16),
                pltpu.VMEM((groups, LANES), F32),
            ],
            compiler_params=params(32768),
        )(received[k], prepared, mix, coefs, *before)

    shift_level = pl.pallas_call(
        functools.partial(shift_kernel, SHIFT_STEP),
        out_shape=pltpu.VMEM((scenarios, groups, LANES), F32),
        in_specs=[VMEM] * 3 + [pl.BlockSpec(memory_space=pl.ANY)],
        out_specs=VMEM,
        cost_estimate=pl.CostEstimate(flops=40_000_000, bytes_accessed=2_000_000, transcendentals=0),
        compiler_params=params(16384),
    )(matrix, prepared, coefs, partial_levels)

    rest = jnp.zeros_like(partial_levels) if n_scen == 1 else None
    hop = 1
    while hop < n_scen:
        if rest is not None:
            partial_levels = partial_levels + rest
        rest = lax.ppermute(partial_levels, "scen", [(i, i ^ hop) for i in range(n_scen)])
        hop *= 2
    return pl.pallas_call(
        value_kernel,
        out_shape=(jax.ShapeDtypeStruct((scenarios, trades), F32),) * 3,
        in_specs=[VMEM] * 4,
        out_specs=(VMEM,) * 3,
        scratch_shapes=[pltpu.VMEM((2 * groups, LANES), F32)],
        compiler_params=params(8192),
    )(partial_levels, rest, shift_level, prepared)


def solution(mesh):
    in_specs = (
        P("trade", None),
        P("trade"),
        P(),
        P("scen"),
        P("trade"),
        P("trade", None),
        P("trade"),
        P("trade"),
        P("trade"),
        P("trade"),
        P("trade"),
        P("trade"),
        P("trade"),
    )
    out_specs = (P("scen", "trade"), P("scen", "trade"), P("scen", "trade"))
    return jax.shard_map(shards, mesh=mesh, in_specs=in_specs, out_specs=out_specs, check_vma=False)
```

```python
import functools

import jax
import jax.numpy as jnp
from jax import lax
from jax.experimental import pallas as pl
from jax.experimental.pallas import tpu as pltpu
from jax.sharding import PartitionSpec as P

NE = 64
NK = 32
HOT = 2
LANES = 128
BAND = 8
BLOCKS = NE // BAND
TILES = BAND * NK // LANES
WIDE = BAND * NK
REACH = BAND + 3
EXTRA = 16
CENTRE = 1.4
PREPARE_STEP = 32
SHIFT_STEP = 32
SURFACE_STEP = 64

RATE = 0.03
INV_ROOT_TWO = 0.7071067811865476
INV_ROOT_TAU = 0.3989422804014327

VMEM = pl.BlockSpec(memory_space=pltpu.VMEM)
HBM = pl.BlockSpec(memory_space=pltpu.HBM)
F32 = jnp.float32
BF16 = jnp.bfloat16

(WE, FIRST, BLK, SLOT, PICK, BIAS) = (0, 4, 5, 6, 7, 8)
(ROOT, MONEY, GROWTH, CASH, VALUE) = (9, 10, 11, 12, 13)
PREPARED = 14


def spline_weights(offset):
    square = offset * offset
    offset_cube = square * offset
    return (
        0.5 * (2.0 * square - offset_cube - offset),
        0.5 * (3.0 * offset_cube - 5.0 * square + 2.0),
        0.5 * (4.0 * square - 3.0 * offset_cube + offset),
        0.5 * (offset_cube - square),
    )


def in_hbm(*arrays):
    return [pltpu.with_memory_space_constraint(x, pltpu.HBM) if x.size > 1 else x for x in arrays]


def params(kilobytes):
    return pltpu.CompilerParams(vmem_limit_bytes=kilobytes << 10)


def pack_kernel(hot_in, log_vol_in, beta_in, out_ref, log_vol_ref, beta_ref, hot_ref, sems, small):
    owned = log_vol_ref.shape[0]
    per_tile = LANES // owned
    steps = BLOCKS // per_tile
    width = log_vol_ref.shape[1] // steps
    copies = []
    for tile in range(steps):
        columns = pl.ds(tile * width, width)
        copies.append(
            pltpu.make_async_copy(
                log_vol_in.at[:, columns], log_vol_ref.at[:, columns], sems.at[tile]
            )
        )
    copies.append(pltpu.make_async_copy(beta_in, beta_ref, small.at[0]))
    copies.append(pltpu.make_async_copy(hot_in, hot_ref, small.at[1]))
    for copy in copies:
        copy.start()
    for tile in range(steps):
        copies[tile].wait()
        for half in range(TILES):
            first = [((tile * per_tile + i) * TILES + half) * LANES for i in range(per_tile)]
            stacked = jnp.concatenate([log_vol_ref[:, c : c + LANES] for c in first], axis=0)
            out_ref[half * LANES : (half + 1) * LANES, tile * LANES : (tile + 1) * LANES] = (
                jnp.transpose((stacked + CENTRE).astype(BF16))
            )
    copies[steps].wait()
    copies[steps + 1].wait()
    row = lax.broadcasted_iota(jnp.int32, (EXTRA, LANES), 0)
    beta = jnp.broadcast_to(beta_ref[...], (EXTRA, owned))
    high = beta.astype(BF16).astype(F32)
    middle = (beta - high).astype(BF16).astype(F32)
    low = beta - high - middle
    zero = jnp.zeros((EXTRA, LANES), F32)
    row_b = row[:, 0:owned]
    pieces = jnp.where(row_b == 0, high, jnp.where(row_b == 1, middle, jnp.where(row_b == 2, low, 0.0)))
    hots = zero
    for i in range(HOT):
        hots = jnp.where(row == i, hot_ref[i].astype(F32), hots)
    out_ref[WIDE : WIDE + EXTRA, 0:LANES] = zero.astype(BF16)
    out_ref[WIDE : WIDE + EXTRA, 0:owned] = pieces.astype(BF16)
    out_ref[WIDE : WIDE + EXTRA, LANES : 2 * LANES] = hots.astype(BF16)
    for tile in range(2, BLOCKS // per_tile):
        out_ref[WIDE : WIDE + EXTRA, tile * LANES : (tile + 1) * LANES] = zero.astype(BF16)


def placed(position, weights, first, shape):
    distance = position - jnp.broadcast_to(first, shape)
    result = jnp.zeros(shape, F32)
    for tap in range(4):
        result = jnp.where(distance == float(tap), jnp.broadcast_to(weights[tap], shape), result)
    return result


def parity(value, count):
    return sum((value >> i) & 1 for i in range(count.bit_length() - 1)) & 1


def prepare_kernel(
    device_count,
    n_scen,
    owned,
    per_step,
    scen_in,
    shock_ref,
    *refs,
):
    whole, reals = refs[:4], refs[4:8]
    out_ref, mix_ref, coef_ref, matrix_ref = refs[8:12]
    scen_ref, whole_ref, real_ref, rows_ref, wide_ref, row_ref, tap_ref, sems, sem = refs[12:]
    groups = out_ref.shape[1]
    scenarios = rows_ref.shape[0]
    ids = pltpu.make_async_copy(scen_in, scen_ref, sems.at[8])
    ids.start()
    columns = []
    for i in range(4):
        columns.append(pltpu.make_async_copy(whole[i], whole_ref.at[i], sems.at[i]))
        columns.append(pltpu.make_async_copy(reals[i], real_ref.at[i], sems.at[4 + i]))
    for copy in columns:
        copy.start()
    ids.wait()
    copies = []
    for s in range(scenarios):
        first = pl.multiple_of(lax.shift_right_logical(scen_ref[s], 4) * 16, 16)
        copies.append(
            pltpu.make_async_copy(shock_ref.at[pl.ds(first, 16), :], rows_ref.at[s], sem.at[s])
        )
        copies[-1].start()
    for copy in columns:
        copy.wait()
    dest, pick, expiry, strike = [whole_ref[i] for i in range(4)]
    frac_e, frac_k, notional, forward = [real_ref[i] for i in range(4)]
    weights = [w.astype(BF16).astype(F32) for w in spline_weights(frac_e)]
    for tap in range(4):
        out_ref[WE + tap] = weights[tap]
    taps = spline_weights(frac_k)
    for tap in range(4):
        tap_ref[tap] = taps[tap]
    out_ref[BIAS] = CENTRE * (
        (weights[0] + weights[1] + weights[2] + weights[3]) * (taps[0] + taps[1] + taps[2] + taps[3])
    )
    first_row = expiry - 1
    block = lax.shift_right_logical(first_row, BAND.bit_length() - 1)
    row_ref[0] = (first_row - block * BAND).astype(F32)
    row_ref[1] = (strike - 1).astype(F32)
    out_ref[FIRST] = first_row.astype(F32)
    out_ref[BLK] = block.astype(F32)
    hot = pick - owned
    step = jnp.where(hot < 0, 0, jnp.where(hot < HOT, device_count - 1, 1))
    owner = (dest + step) & (device_count - 1)
    offset = owner ^ lax.axis_index("trade")
    scen_place = lax.axis_index("scen")
    ring = lax.shift_right_logical(offset, n_scen.bit_length() - 1)
    mine = ((offset & (n_scen - 1)) ^ ((ring & 1) * (n_scen // 2))) == scen_place
    slot = ring ^ (parity(scen_place, n_scen) & (device_count // n_scen - 1))
    out_ref[SLOT] = jnp.where(mine, slot, -1).astype(F32)
    out_ref[PICK] = jnp.where(hot < HOT, pick, pick - HOT).astype(F32)

    maturity = (expiry.astype(F32) + frac_e + 1.0) * (4.0 / NE)
    moneyness = (strike.astype(F32) + frac_k - 0.5 * (NK - 1)) / NK
    scaled = notional * jnp.exp(-RATE * maturity)
    out_ref[ROOT] = jnp.sqrt(maturity)
    out_ref[MONEY] = moneyness
    out_ref[GROWTH] = jnp.exp(moneyness)
    out_ref[CASH] = scaled
    out_ref[VALUE] = scaled * forward

    strikes = lax.broadcasted_iota(jnp.int32, (NK, LANES), 0).astype(F32)
    expiries = lax.broadcasted_iota(jnp.int32, (2 * BAND, LANES), 0).astype(F32)

    def some(i, carry):
        for part in range(per_step):
            g = i * per_step + part
            columns = pl.ds(pl.multiple_of(g * LANES, LANES), LANES)
            taps = [out_ref[WE + tap, pl.ds(g, 1), :] for tap in range(4)]
            mix_ref[:, columns] = placed(
                expiries, taps, row_ref[0, pl.ds(g, 1), :], (2 * BAND, LANES)
            )
            taps = [tap_ref[tap, pl.ds(g, 1), :] for tap in range(4)]
            coef_ref[:, columns] = placed(strikes, taps, row_ref[1, pl.ds(g, 1), :], (NK, LANES))
        return carry

    lax.fori_loop(0, groups // per_step, some, 0)

    tiles = NE * NK // LANES
    in_tile = LANES // NK
    line = lax.broadcasted_iota(jnp.int32, (16, NE * NK), 0)
    for s in range(scenarios):
        copies[s].wait()
        wanted = jnp.where(line == (scen_ref[s] & 15), rows_ref[s].astype(F32), 0.0)
        wanted = jnp.sum(wanted, axis=0, keepdims=True)
        stacked = jnp.concatenate(
            [wanted[:, i * LANES : (i + 1) * LANES] for i in range(tiles)], axis=0
        )
        turned = jnp.transpose(stacked)
        for i in range(in_tile):
            wide_ref[s * NK : (s + 1) * NK, i * tiles : (i + 1) * tiles] = turned[
                i * NK : (i + 1) * NK, :
            ]
    matrix_ref[...] = wide_ref[...].astype(BF16)


def shift_kernel(per_step, matrix_ref, pre_ref, coef_ref, after_ref, shift_ref):
    scenarios, groups = shift_ref.shape[0], shift_ref.shape[1]
    tiles = NE * NK // LANES
    in_tile = LANES // NK
    shift = matrix_ref[...]
    place = lax.broadcasted_iota(jnp.int32, (NE, LANES), 0)
    expiries = (
        (place & (tiles - 1)) * in_tile + lax.shift_right_logical(place, tiles.bit_length() - 1)
    ).astype(F32)

    def some(i, carry):
        sides = []
        for part in range(per_step):
            g = i * per_step + part
            taps = [pre_ref[WE + tap, pl.ds(g, 1), :] for tap in range(4)]
            sides.append(
                placed(expiries, taps, pre_ref[FIRST, pl.ds(g, 1), :], (NE, LANES)).astype(BF16)
            )
        mixed = jnp.dot(shift, jnp.concatenate(sides, axis=1), preferred_element_type=F32)
        for part in range(per_step):
            g = i * per_step + part
            coefs = coef_ref[:, pl.ds(pl.multiple_of(g * LANES, LANES), LANES)]
            for s in range(scenarios):
                piece = mixed[s * NK : (s + 1) * NK, part * LANES : (part + 1) * LANES]
                shift_ref[s, pl.ds(g, 1), :] = jnp.sum(piece * coefs, axis=0, keepdims=True)
        return carry

    lax.fori_loop(0, groups // per_step, some, 0)


def surface_kernel(slot, owned, per_step, message_ref, pre_ref, mix_ref, coef_ref, *refs):
    before_ref = refs[0] if len(refs) == 5 else None
    out_ref, total_ref, table_ref, index_ref = refs[-4:]
    groups = pre_ref.shape[1]
    if before_ref is not None:
        total_ref[...] = before_ref[...].astype(F32)
    table_ref[0:WIDE, :] = message_ref[0:WIDE, :]
    table_ref[WIDE : WIDE + 3 * NK, :] = pltpu.roll(
        message_ref[0 : 3 * NK, :].astype(F32), (BLOCKS - 1) * owned, 1
    ).astype(BF16)
    extra = message_ref[WIDE : WIDE + EXTRA, 0 : 2 * LANES].astype(F32)
    betas = extra[0:1, 0:LANES] + extra[1:2, 0:LANES] + extra[2:3, 0:LANES]
    sub = 8
    for i in range(groups // sub):
        rows = pl.ds(i * sub, sub)
        held = pre_ref[SLOT, rows, :] == float(slot)
        local = pre_ref[PICK, rows, :]
        for h in range(HOT):
            hot = jnp.broadcast_to(extra[h : h + 1, LANES : 2 * LANES], (sub, LANES))
            local = jnp.where(local == float(owned + h), hot, local)
        looked = jnp.take_along_axis(
            jnp.broadcast_to(betas, (sub, LANES)),
            local.astype(jnp.int32),
            axis=1,
            mode="promise_in_bounds",
        )
        index_ref[rows, :] = jnp.where(held, local, -1.0)
        later = pl.ds(groups + i * sub, sub)
        other = 0.0 if before_ref is None else total_ref[later, :]
        total_ref[later, :] = jnp.where(held, looked, other)

    underlyings = lax.broadcasted_iota(jnp.int32, (owned, LANES), 0).astype(F32)
    zero = jnp.zeros((owned, LANES), BF16)

    def some(i, carry):
        sides = []
        for part in range(per_step):
            g = i * per_step + part
            index = jnp.broadcast_to(index_ref[pl.ds(g, 1), :], (owned, LANES))
            chosen = jnp.where(underlyings == index, 1.0, 0.0).astype(BF16)
            block = jnp.broadcast_to(pre_ref[BLK, pl.ds(g, 1), :], (owned, LANES)).astype(BF16)
            sides.append(
                jnp.concatenate(
                    [
                        jnp.where(block == jnp.asarray(j, BF16), chosen, zero)
                        for j in range(BLOCKS)
                    ],
                    axis=0,
                )
            )
        product = jnp.dot(
            table_ref[...], jnp.concatenate(sides, axis=1), preferred_element_type=F32
        )
        for part in range(per_step):
            g = i * per_step + part
            columns = slice(part * LANES, (part + 1) * LANES)
            here = pl.ds(pl.multiple_of(g * LANES, LANES), LANES)
            mix = mix_ref[:, here]
            curve = jnp.zeros((NK, LANES), F32)
            for a in range(REACH):
                curve = curve + product[a * NK : (a + 1) * NK, columns] * mix[a : a + 1, :]
            level = jnp.sum(curve * coef_ref[:, here], axis=0, keepdims=True)
            held = index_ref[pl.ds(g, 1), :] >= 0.0
            other = 0.0 if before_ref is None else total_ref[pl.ds(g, 1), :]
            total_ref[pl.ds(g, 1), :] = jnp.where(held, level, other)
        return carry

    lax.fori_loop(0, groups // per_step, some, 0)
    out_ref[...] = total_ref[...].astype(BF16)


def value_kernel(
    part_ref, rest_ref, shift_ref, pre_ref, price_ref, vega_ref, delta_ref, total_ref
):
    total_ref[...] = part_ref[...].astype(F32) + rest_ref[...].astype(F32)
    scenarios, groups = shift_ref.shape[0], shift_ref.shape[1]
    sub = 8
    for i in range(groups // sub):
        rows = pl.ds(i * sub, sub)
        later = pl.ds(groups + i * sub, sub)
        level = total_ref[rows, :] - pre_ref[BIAS, rows, :]
        slope = total_ref[later, :]
        root_time = pre_ref[ROOT, rows, :]
        moneyness = pre_ref[MONEY, rows, :]
        growth = pre_ref[GROWTH, rows, :]
        scaled = pre_ref[CASH, rows, :]
        value = pre_ref[VALUE, rows, :]
        results = ([], [], [])
        for s in range(scenarios):
            spread = jnp.exp(level + slope * shift_ref[s, rows, :]) * root_time
            upper_d = -moneyness / spread + 0.5 * spread
            lower_d = upper_d - spread
            cdf_upper = 0.5 + 0.5 * lax.erf(upper_d * INV_ROOT_TWO)
            cdf_lower = 0.5 + 0.5 * lax.erf(lower_d * INV_ROOT_TWO)
            results[0].append(value * (cdf_upper - growth * cdf_lower))
            results[1].append(value * INV_ROOT_TAU * jnp.exp(-0.5 * upper_d * upper_d) * root_time)
            results[2].append(scaled * cdf_upper)
        for r in range(sub):
            columns = pl.ds((i * sub + r) * LANES, LANES)
            for ref, result in zip((price_ref, vega_ref, delta_ref), results):
                ref[:, columns] = jnp.concatenate([x[r : r + 1, :] for x in result], axis=0)


def shards(
    log_vol,
    beta,
    shock_table,
    scen_ids,
    hot_index,
    dest,
    pick,
    expiry_cell,
    strike_cell,
    frac_e,
    frac_k,
    notional,
    forward,
):
    n_trade = lax.axis_size("trade")
    n_scen = lax.axis_size("scen")
    slots = n_trade // n_scen
    owned = log_vol.shape[0]
    trades = pick.shape[0]
    groups = trades // LANES
    scenarios = scen_ids.shape[0]

    message = pl.pallas_call(
        pack_kernel,
        out_shape=pltpu.VMEM((WIDE + EXTRA, BLOCKS * owned), BF16),
        in_specs=[HBM] * 3,
        out_specs=VMEM,
        scratch_shapes=[
            pltpu.VMEM(log_vol.shape, F32),
            pltpu.VMEM((1, owned), F32),
            pltpu.SMEM(hot_index.shape, jnp.int32),
            pltpu.SemaphoreType.DMA((BLOCKS * owned // LANES,)),
            pltpu.SemaphoreType.DMA((2,)),
        ],
        compiler_params=params(16384),
    )(*in_hbm(hot_index, log_vol, beta.reshape(1, owned)))

    received = [None] * slots
    for k in reversed(range(slots)):
        pairs = []
        for d in range(n_trade):
            for q in range(n_scen):
                ring = k ^ (parity(q, n_scen) & (slots - 1))
                offset = ring * n_scen + (q ^ ((ring & 1) * (n_scen // 2)))
                pairs.append(((d ^ offset) * n_scen + q, d * n_scen + q))
        received[k] = lax.ppermute(message, ("trade", "scen"), pairs)

    dense = [
        column.reshape(groups, LANES)
        for column in (
            dest,
            pick,
            expiry_cell,
            strike_cell,
            frac_e,
            frac_k,
            notional,
            forward,
        )
    ]
    prepared, mix, coefs, matrix = pl.pallas_call(
        functools.partial(prepare_kernel, n_trade, n_scen, owned, PREPARE_STEP),
        out_shape=(
            pltpu.VMEM((PREPARED, groups, LANES), F32),
            pltpu.VMEM((2 * BAND, trades), F32),
            pltpu.VMEM((NK, trades), F32),
            pltpu.VMEM((scenarios * NK, NE), BF16),
        ),
        in_specs=[HBM] * 10,
        out_specs=(VMEM,) * 4,
        scratch_shapes=[
            pltpu.SMEM(scen_ids.shape, jnp.int32),
            pltpu.VMEM((4, groups, LANES), jnp.int32),
            pltpu.VMEM((4, groups, LANES), F32),
            pltpu.VMEM((scenarios, 16, NE * NK), BF16),
            pltpu.VMEM((scenarios * NK, NE), F32),
            pltpu.VMEM((2, groups, LANES), F32),
            pltpu.VMEM((4, groups, LANES), F32),
            pltpu.SemaphoreType.DMA((9,)),
            pltpu.SemaphoreType.DMA((scenarios,)),
        ],
        cost_estimate=pl.CostEstimate(flops=40_000_000, bytes_accessed=6_000_000, transcendentals=0),
        compiler_params=params(16384),
    )(*in_hbm(scen_ids, shock_table, *dense))

    partial_levels = None
    for k in reversed(range(slots)):
        before = [] if partial_levels is None else [partial_levels]
        partial_levels = pl.pallas_call(
            functools.partial(surface_kernel, k, owned, SURFACE_STEP),
            out_shape=jax.ShapeDtypeStruct((2 * groups, LANES), BF16),
            in_specs=[VMEM] * (4 + len(before)),
            out_specs=VMEM,
            scratch_shapes=[
                pltpu.VMEM((2 * groups, LANES), F32),
                pltpu.VMEM((WIDE + 3 * NK, BLOCKS * owned), BF16),
                pltpu.VMEM((groups, LANES), F32),
            ],
            compiler_params=params(32768),
        )(received[k], prepared, mix, coefs, *before)

    shift_level = pl.pallas_call(
        functools.partial(shift_kernel, SHIFT_STEP),
        out_shape=pltpu.VMEM((scenarios, groups, LANES), F32),
        in_specs=[VMEM] * 3 + [pl.BlockSpec(memory_space=pl.ANY)],
        out_specs=VMEM,
        cost_estimate=pl.CostEstimate(flops=40_000_000, bytes_accessed=2_000_000, transcendentals=0),
        compiler_params=params(16384),
    )(matrix, prepared, coefs, partial_levels)

    rest = jnp.zeros_like(partial_levels) if n_scen == 1 else None
    hop = 1
    while hop < n_scen:
        if rest is not None:
            partial_levels = partial_levels + rest
        rest = lax.ppermute(partial_levels, "scen", [(i, i ^ hop) for i in range(n_scen)])
        hop *= 2
    return pl.pallas_call(
        value_kernel,
        out_shape=(jax.ShapeDtypeStruct((scenarios, trades), F32),) * 3,
        in_specs=[VMEM] * 4,
        out_specs=(VMEM,) * 3,
        scratch_shapes=[pltpu.VMEM((2 * groups, LANES), F32)],
        compiler_params=params(8192),
    )(partial_levels, rest, shift_level, prepared)


def solution(mesh):
    in_specs = (
        P("trade", None),
        P("trade"),
        P(),
        P("scen"),
        P("trade"),
        P("trade", None),
        P("trade"),
        P("trade"),
        P("trade"),
        P("trade"),
        P("trade"),
        P("trade"),
        P("trade"),
    )
    out_specs = (P("scen", "trade"), P("scen", "trade"), P("scen", "trade"))
    return jax.shard_map(shards, mesh=mesh, in_specs=in_specs, out_specs=out_specs, check_vma=False)
```
